32 devices in a mesh: seq: 8 (over z, x), mp: 4 (over y, core).
Axes of the slice: x: 2, y: 2, z: 4, core: 2. Of those that a mesh axis runs over, the one named last changes fastest.
Arguments:
- hidden_in: bfloat16 [32, 2048], P('mp'), may hold values from -24 to 24
- query_weight: bfloat16 [2048, 3072], P(None, 'seq'), may hold values from -0.25 to 0.25
- key_absorb: bfloat16 [16, 128, 512], replicated, may hold values from -0.5 to 0.5
- value_up: bfloat16 [16, 512, 128], replicated, may hold values from -0.25 to 0.25
- out_weight: bfloat16 [2048, 2048], P(None, 'seq'), may hold values from -0.5 to 0.5
- latent_cache: bfloat16 [32, 1024, 576], P('mp', 'seq'), may hold values from -41 to 41
- cache_lengths: int32 [32], P('mp'), may hold values from 128 to 1024, as said below
- keep_lists: int32 [32, 8, 64], P('mp', 'seq'), may hold values from 0 to 127, as said below
- drop_weights: int32 [32, 1024], P('mp', 'seq'), may hold values from 1 to 8
- pack_dest: int32 [32, 8], P('mp'), may hold values from -1 to 31, as said below
- final_gain: bfloat16 [2048], replicated, may hold values from 0.5 to 1.5
- head_weight: bfloat16 [2048, 102400], P(None, ('seq', 'mp')), may hold values from -0.125 to 0.125
- tenant_ranges: int32 [4, 2], replicated, may hold values from 0 to 102400, as said below
- tenant_ids: int32 [32], replicated, may hold values from 0 to 3
Outputs:
- packed_rows: bfloat16 [128, 64, 576], P(('seq', 'mp'))
- packed_summary: bfloat16 [128, 576], P(('seq', 'mp'))
- hidden_out: bfloat16 [32, 2048], P('mp', 'seq')
- state_norm: float32 [32], P('mp')
- top_logit: float32 [32], P('mp')
The draws below stay inside these ranges and needn't reach their ends.
Inputs may be any that keep to these rules, and one draw needn't show every extreme that they name: `cache_lengths`: every length is a whole number of 128-position blocks, at least one block. Within each group of 8 requests (one index of mp) the lengths add up to 4096, and some request of the group has the full 1024. `keep_lists`: the 64 positions of a block are distinct and ascending. pack_dest[r, b] is -1 exactly when block b of request r is not live; otherwise it is owner * 4 + slot with an owner in 0 to 8 - 1 (an index of seq) and a slot in 0 to 3. Within one group of 8 requests the live blocks take every destination exactly once. Of the live blocks of one block index in one group, at most 1 go to any one owner, and those that share an owner take consecutive slots. Block index 0 is live for every request of a group, and some owner receives 1 of them. `tenant_ranges`: row t is tenant t's window [low, high) of vocabulary entries; each window holds at least 51200 entries.
All inputs are finite; a program needn't handle non-finite values.
Results may differ from the reference program's by a relative error of at most 0.0075.
Values may be sent and summed in bfloat16 or wider, within the bound.
A program may use at most 128 MiB of HBM per device.

```python
import jax
import jax.numpy as jnp
from jax import lax

D = 2048
H = 16
NOPE = 128
ROPE = 64
LAT = 512
VH = 128
V = 102400
BLK = 128
KB = 64
TENANTS = 4
RQ = 8
R = 32
NB = 8
MAXLEN = 1024
SLOTS = 4
POOL = 128
N_MP = 4


def block_counts(key):
    half_blocks = NB // 2

    def one_group(group_key):
        spread_key, order_key = jax.random.split(group_key)
        spread_draw = jax.random.randint(spread_key, (RQ // 2 - 2,), -(half_blocks - 1), half_blocks)
        paired = jnp.stack([half_blocks + spread_draw, half_blocks - spread_draw], axis=1).reshape(-1)
        leading = jnp.array([NB, 1, half_blocks - 1, half_blocks], dtype=jnp.int32)
        counts = jnp.concatenate([leading, paired.astype(jnp.int32)])
        return counts[jax.random.permutation(order_key, RQ)]
    return jax.vmap(one_group)(jax.random.split(key, R // RQ))


def draw_cache_lengths(key, part):
    return (block_counts(jax.random.fold_in(key, 11)) * BLK).reshape(R).astype(jnp.int32)


def draw_pack_dest(key, part):
    counts = block_counts(jax.random.fold_in(key, 11))
    slot_count = RQ // 2

    def one_group(counts_row, group_key):
        order_key, owner_key = jax.random.split(group_key)
        priority = jnp.argsort(jax.random.permutation(order_key, RQ)).astype(jnp.int32)
        live_mask = (jnp.arange(NB, dtype=jnp.int32)[None, :] < counts_row[:, None]).astype(jnp.int32)
        per_source = jnp.sum(live_mask, axis=0)
        offsets = jnp.cumsum(per_source) - per_source
        before = (priority[None, :] < priority[:, None]).astype(jnp.int32)
        within = jnp.matmul(before, live_mask)
        order_rank = offsets[None, :] + within
        owners = jax.random.permutation(owner_key, NB).astype(jnp.int32)
        destination = owners[order_rank % NB] * slot_count + order_rank // NB
        return jnp.where(live_mask > 0, destination, -1)
    group_keys = jax.random.split(jax.random.fold_in(key, 23), R // RQ)
    return jax.vmap(one_group)(counts, group_keys).reshape(R, NB).astype(jnp.int32)


def draw_keep_lists(key, part):
    scores = jax.random.randint(key, (R, NB, BLK), 0, 1 << 20) * BLK + jnp.arange(BLK, dtype=jnp.int32)
    chosen = jnp.argsort(scores, axis=-1)[..., :KB]
    return jnp.sort(chosen, axis=-1).astype(jnp.int32)


def draw_tenant_ranges(key, part):
    low_key, span_key = jax.random.split(key)
    tenant_index = jnp.arange(TENANTS, dtype=jnp.int32)
    window_low = jax.random.randint(low_key, (TENANTS,), 0, V // 4 + 1)
    window_low = jnp.where(tenant_index == 0, 0, window_low)
    window_span = jax.random.randint(span_key, (TENANTS,), V // 2, 3 * V // 4 + 1)
    window_high = jnp.where(tenant_index == 1, V, window_low + window_span)
    return jnp.stack([window_low, window_high], axis=1).astype(jnp.int32)


def draw_hidden_in(key, part):
    value_key, offset_key = jax.random.split(jax.random.fold_in(key, 5))
    base = jnp.clip(jax.random.normal(value_key, (R, D), jnp.float32), -6.0, 6.0) * 0.5
    offset = jax.random.randint(offset_key, (), 0, NB)
    heavy_block = (jnp.arange(R, dtype=jnp.int32) + offset) % NB
    column_block = jnp.arange(D, dtype=jnp.int32) // (D // NB)
    factor = jnp.where(column_block[None, :] == heavy_block[:, None], 8.0, 1.0)
    return (base * factor).astype(jnp.bfloat16)


def draw_latent_cache(key, part):
    shape_full = (R, MAXLEN, LAT + ROPE)
    value_key = jax.random.fold_in(key, 0)
    sign_key = jax.random.fold_in(key, 2)
    level_key = jax.random.fold_in(key, 3)
    values_base = jnp.clip(jax.random.normal(value_key, shape_full, jnp.float32), -6.0, 6.0)
    pattern = jnp.where(jax.random.randint(sign_key, (1, 1, LAT + ROPE), 0, 2) == 0, -1.0, 1.0)
    spiked = jax.random.randint(level_key, (R, MAXLEN, 1), 0, 64)
    level = jnp.where(spiked == 0, 41.0, 38.0)
    return jnp.where(spiked < 2, level * pattern, values_base).astype(jnp.bfloat16)


def with_ends(entries, rng, least, largest):
    longest = entries.shape.index(max(entries.shape))
    spots = []
    for shift in (0, 1):
        where = [jax.random.randint(jax.random.fold_in(rng, axis), (), 0, length) for axis, length in enumerate(entries.shape)]
        where[longest] = (where[longest] + shift) % entries.shape[longest]
        spots.append(tuple(where))
    return entries.at[spots[0]].set(least).at[spots[1]].set(largest)


def levels(key, extent, shards, smallest, high):
    loudness = 1.0
    for position, blocks in shards:
        steps = jax.random.uniform(jax.random.fold_in(jax.random.fold_in(key, 6), position), (blocks,), jnp.float32, smallest / len(shards), high / len(shards))
        loudness = loudness * jnp.repeat(jnp.exp(steps), extent[position] // blocks).reshape((-1,) + (1,) * (len(extent) - 1 - position))
    return loudness


def scatter_about(own_key, shape, scale, most, cuts=(), kind=jnp.bfloat16):
    drawn = scale * jax.random.normal(own_key, shape, jnp.float32)
    if cuts:
        drawn = drawn * levels(own_key, shape, cuts, -0.22, 0.18)
    return jnp.clip(drawn, -most, most).astype(kind)


def setup_inputs(seed: int = 0) -> dict:
    key_of = jax.random.split(jax.random.key(seed), 15)
    return {
        "hidden_in": draw_hidden_in(jax.random.fold_in(key_of[14], 71), 0),
        "query_weight": scatter_about(key_of[1], (D, H * (NOPE + ROPE)), (D // 4) ** -0.5, 0.25, ((1, 8),)),
        "key_absorb": scatter_about(key_of[2], (H, NOPE, LAT), NOPE ** -0.5, 0.5),
        "value_up": scatter_about(key_of[3], (H, LAT, VH), LAT ** -0.5, 0.25),
        "out_weight": scatter_about(key_of[4], (H * VH, D), (H * VH // 16) ** -0.5, 0.5, ((1, 8),)),
        "latent_cache": draw_latent_cache(jax.random.fold_in(key_of[14], 71), 0),
        "cache_lengths": draw_cache_lengths(jax.random.fold_in(key_of[14], 71), 0),
        "keep_lists": draw_keep_lists(jax.random.fold_in(key_of[14], 71), 0),
        "drop_weights": with_ends(jax.random.randint(key_of[8], (R, MAXLEN), 1, 9), jax.random.fold_in(key_of[8], 1), 1, 8).astype(jnp.int32),
        "pack_dest": draw_pack_dest(jax.random.fold_in(key_of[14], 71), 0),
        "final_gain": jnp.clip(1.0 + 0.1 * jax.random.normal(key_of[10], (D,), jnp.float32), 0.5, 1.5).astype(jnp.bfloat16),
        "head_weight": scatter_about(key_of[11], (D, V), D ** -0.5, 0.125, ((1, 32),)),
        "tenant_ranges": draw_tenant_ranges(jax.random.fold_in(key_of[14], 71), 0),
        "tenant_ids": with_ends(jax.random.randint(key_of[13], (R,), 0, TENANTS), jax.random.fold_in(key_of[13], 1), 0, TENANTS - 1).astype(jnp.int32),
    }


NEGATIVE = -1e+30
HIGHEST = lax.Precision.HIGHEST

def compact_request(cache_rows, keep_rows, weight_rows):
    blocks = cache_rows.reshape(NB, BLK, LAT + ROPE)
    kept_rows = jnp.take_along_axis(blocks, keep_rows[:, :, None], axis=1)
    positions = jnp.arange(BLK, dtype=jnp.int32)
    kept_flag = lax.optimization_barrier(jnp.sum((keep_rows[:, :, None] == positions[None, None, :]).astype(jnp.float32), axis=1))
    weights_dropped = weight_rows.reshape(NB, BLK).astype(jnp.float32) * (1.0 - kept_flag)
    weight_mass = lax.optimization_barrier(jnp.sum(weights_dropped, axis=1))
    summed = jnp.einsum('bt,btc->bc', weights_dropped, blocks.astype(jnp.float32), precision=HIGHEST)
    summary = (summed / weight_mass[:, None]).astype(jnp.bfloat16)
    return (kept_rows, summary)

def attend_request(query_lat, query_rope, kept_rows, summary, live_blocks):
    score_scale = (NOPE + ROPE) ** (-0.5)
    key_lat = kept_rows[:, :, :LAT].astype(jnp.float32)
    key_rope = kept_rows[:, :, LAT:].astype(jnp.float32)
    lat_query = query_lat.astype(jnp.float32)
    rope_query = query_rope.astype(jnp.float32)
    summary_f = summary.astype(jnp.float32)
    row_scores = (jnp.einsum('hl,bkl->hbk', lat_query, key_lat, precision=HIGHEST) + jnp.einsum('hr,bkr->hbk', rope_query, key_rope, precision=HIGHEST)) * score_scale
    summ_scores = (jnp.einsum('hl,bl->hb', lat_query, summary_f[:, :LAT], precision=HIGHEST) + jnp.einsum('hr,br->hb', rope_query, summary_f[:, LAT:], precision=HIGHEST)) * score_scale
    summ_scores = summ_scores + jnp.log(jnp.float32(BLK - KB))
    row_scores = jnp.where(live_blocks[None, :, None], row_scores, NEGATIVE)
    summ_scores = jnp.where(live_blocks[None, :], summ_scores, NEGATIVE)
    maxima = jnp.maximum(lax.optimization_barrier(jnp.max(row_scores, axis=(1, 2))), lax.optimization_barrier(jnp.max(summ_scores, axis=1)))
    row_weights = jnp.where(live_blocks[None, :, None], jnp.exp(row_scores - maxima[:, None, None]), 0.0)
    summ_weights = jnp.where(live_blocks[None, :], jnp.exp(summ_scores - maxima[:, None]), 0.0)
    totals = lax.optimization_barrier(jnp.sum(row_weights, axis=(1, 2))) + lax.optimization_barrier(jnp.sum(summ_weights, axis=1))
    weighted = jnp.einsum('hbk,bkl->hl', row_weights, key_lat, precision=HIGHEST) + jnp.einsum('hb,bl->hl', summ_weights, summary_f[:, :LAT], precision=HIGHEST)
    return (weighted / totals[:, None]).astype(jnp.bfloat16)

def reference(hidden_in, query_weight, key_absorb, value_up, out_weight, latent_cache, cache_lengths, keep_lists, drop_weights, pack_dest, final_gain, head_weight, tenant_ranges, tenant_ids):
    query_full = jnp.dot(hidden_in, query_weight, preferred_element_type=jnp.float32).astype(jnp.bfloat16)
    query_full = query_full.reshape(R, H, NOPE + ROPE)
    query_nope = query_full[:, :, :NOPE]
    query_rope = query_full[:, :, NOPE:]
    query_latent = jnp.einsum('rhn,hnl->rhl', query_nope.astype(jnp.float32), key_absorb.astype(jnp.float32), precision=HIGHEST).astype(jnp.bfloat16)

    def per_request(inputs):
        cache_rows, keep_rows, weight_rows, length_row, lat_row, rope_row = inputs
        kept_rows, summary = compact_request(cache_rows, keep_rows, weight_rows)
        live_blocks = jnp.arange(NB, dtype=jnp.int32) * BLK < length_row
        attended = attend_request(lat_row, rope_row, kept_rows, summary, live_blocks)
        return (kept_rows, summary, attended)
    kept_all, summary_all, attended = lax.map(per_request, (latent_cache, keep_lists, drop_weights, cache_lengths, query_latent, query_rope))
    group_index = (jnp.arange(R, dtype=jnp.int32) // RQ)[:, None]
    owner_index = pack_dest // SLOTS
    slot_index = pack_dest % SLOTS
    where_to = jnp.where(pack_dest >= 0, (owner_index * N_MP + group_index) * SLOTS + slot_index, POOL).astype(jnp.int32)
    packed_rows = jnp.zeros((POOL, KB, LAT + ROPE), jnp.bfloat16).at[where_to.reshape(-1)].set(kept_all.reshape(-1, KB, LAT + ROPE), mode='drop')
    packed_summary = jnp.zeros((POOL, LAT + ROPE), jnp.bfloat16).at[where_to.reshape(-1)].set(summary_all.reshape(-1, LAT + ROPE), mode='drop')
    values = jnp.einsum('rhl,hlv->rhv', attended.astype(jnp.float32), value_up.astype(jnp.float32), precision=HIGHEST)
    values = values.astype(jnp.bfloat16).reshape(R, H * VH)
    hidden_out = (hidden_in.astype(jnp.float32) + jnp.dot(values, out_weight, preferred_element_type=jnp.float32)).astype(jnp.bfloat16)
    rows_f = hidden_out.astype(jnp.float32)
    mean_sq = lax.optimization_barrier(jnp.mean(rows_f * rows_f, axis=1))
    state_norm = jnp.sqrt(mean_sq)
    normed = (rows_f * lax.rsqrt(mean_sq + 1e-06)[:, None] * final_gain.astype(jnp.float32)[None, :]).astype(jnp.bfloat16)
    logits = jnp.dot(normed, head_weight, preferred_element_type=jnp.float32)
    window_low = tenant_ranges[tenant_ids, 0]
    window_high = tenant_ranges[tenant_ids, 1]
    columns = jnp.arange(V, dtype=jnp.int32)
    allowed = (columns[None, :] >= window_low[:, None]) & (columns[None, :] < window_high[:, None])
    top_logit = lax.optimization_barrier(jnp.max(jnp.where(allowed, logits, NEGATIVE), axis=1))
    return (packed_rows, packed_summary, hidden_out, state_norm, top_logit)
```

```python
import functools

import jax
import jax.numpy as jnp
from jax import lax
from jax.experimental import pallas as pl
from jax.experimental.pallas import tpu as pltpu
from jax.sharding import PartitionSpec as P

H = 16
NOPE = 128
ROPE = 64
LAT = 512
VH = 128
BLK = 128
KB = 64
TENANTS = 4
RQ = 8


NEGATIVE = -1e30
HIGHEST = lax.Precision.HIGHEST


def merged(x, axis, combine):
    everything = jax.tree.map(lambda part: lax.all_gather(part, axis), x)
    initial = jax.tree.map(lambda part: part[0], everything)

    def step(k, so_far):
        return combine(so_far, jax.tree.map(lambda part: part[k], everything))

    return lax.fori_loop(1, lax.axis_size(axis), step, initial)


def compact_blocks(block_rows, keep_onehot, weights_dropped):
    kept_rows = jnp.einsum(
        "nkt,ntc->nkc", keep_onehot, block_rows, preferred_element_type=jnp.float32
    ).astype(jnp.bfloat16)
    weight_mass = jnp.sum(weights_dropped.astype(jnp.float32), axis=1)
    summed = jnp.einsum(
        "nt,ntc->nc", weights_dropped, block_rows, preferred_element_type=jnp.float32
    )
    summary = (summed / weight_mass[:, None]).astype(jnp.bfloat16)
    return (kept_rows, summary)


def attend_blocks(query_lat, query_rope, kept_rows, summary, usable):
    score_scale = (NOPE + ROPE) ** (-0.5)
    row_scores = (
        jnp.einsum(
            "nhl,nkl->nhk", query_lat, kept_rows[:, :, :LAT], preferred_element_type=jnp.float32
        )
        + jnp.einsum(
            "nhr,nkr->nhk", query_rope, kept_rows[:, :, LAT:], preferred_element_type=jnp.float32
        )
    ) * score_scale
    summ_scores = (
        jnp.einsum("nhl,nl->nh", query_lat, summary[:, :LAT], preferred_element_type=jnp.float32)
        + jnp.einsum("nhr,nr->nh", query_rope, summary[:, LAT:], preferred_element_type=jnp.float32)
    ) * score_scale
    summ_scores = summ_scores + jnp.log(jnp.float32(BLK - KB))
    row_scores = jnp.where(usable[:, None, None], row_scores, NEGATIVE)
    summ_scores = jnp.where(usable[:, None], summ_scores, NEGATIVE)
    maxima = jnp.maximum(jnp.max(row_scores, axis=2), summ_scores)
    row_weights = jnp.where(usable[:, None, None], jnp.exp(row_scores - maxima[:, :, None]), 0.0)
    summ_weights = jnp.where(usable[:, None], jnp.exp(summ_scores - maxima), 0.0)
    totals = jnp.sum(row_weights, axis=2) + summ_weights
    weighted = jnp.einsum(
        "nhk,nkl->nhl", row_weights, kept_rows[:, :, :LAT].astype(jnp.float32), precision=HIGHEST
    )
    weighted = weighted + summ_weights[:, :, None] * summary[:, None, :LAT].astype(jnp.float32)
    return (maxima, totals, weighted)


def per_request(maxima, totals, weighted, owner_of):
    request_max = jnp.max(jnp.where(owner_of[:, :, None], maxima[None, :, :], NEGATIVE), axis=1)
    shifted = jnp.where(owner_of[:, :, None], maxima[None, :, :] - request_max[:, None, :], 0.0)
    factor = jnp.where(owner_of[:, :, None], jnp.exp(shifted), 0.0)
    request_total = jnp.einsum("rnh,nh->rh", factor, totals, precision=HIGHEST)
    request_sum = jnp.einsum("rnh,nhl->rhl", factor, weighted, precision=HIGHEST)
    return (request_max, request_total, request_sum)


def combine_partial(former, latter):
    former_max, former_total, former_sum = former
    latter_max, latter_total, latter_sum = latter
    joined = jnp.maximum(former_max, latter_max)
    former_factor = jnp.exp(former_max - joined)
    latter_factor = jnp.exp(latter_max - joined)
    return (
        joined,
        former_factor * former_total + latter_factor * latter_total,
        former_factor[:, :, None] * former_sum + latter_factor[:, :, None] * latter_sum,
    )


def body(
    hidden_in,
    query_weight,
    key_absorb,
    value_up,
    out_weight,
    latent_cache,
    cache_lengths,
    keep_lists,
    drop_weights,
    pack_dest,
    final_gain,
    head_weight,
    tenant_ranges,
    tenant_ids,
):
    seq_count = lax.axis_size("seq")
    mp_count = lax.axis_size("mp")
    seq_index = lax.axis_index("seq")
    mp_index = lax.axis_index("mp")
    capacity = max(1, RQ // seq_count)
    slot_count = RQ // 2
    row_width = LAT + ROPE
    query_part = jnp.dot(hidden_in, query_weight, preferred_element_type=jnp.float32).astype(
        jnp.bfloat16
    )
    query_full = lax.all_gather(query_part, "seq", axis=1, tiled=True).reshape(RQ, H, NOPE + ROPE)
    query_lat = jnp.einsum(
        "rhn,hnl->rhl", query_full[:, :, :NOPE], key_absorb, preferred_element_type=jnp.float32
    ).astype(jnp.bfloat16)
    query_rope = query_full[:, :, NOPE:]
    positions = jnp.arange(BLK, dtype=jnp.int32)
    keep_onehot = keep_lists[:, 0, :, None] == positions[None, None, :]
    kept_flag = jnp.sum(keep_onehot.astype(jnp.int32), axis=1)
    weights_dropped = (drop_weights * (1 - kept_flag)).astype(jnp.bfloat16)
    live_here = cache_lengths > seq_index * BLK
    dest_here = lax.dynamic_slice_in_dim(pack_dest, seq_index, 1, 1)[:, 0]
    send_slot = dest_here // slot_count * capacity + dest_here % slot_count % capacity
    slot_range = jnp.arange(seq_count * capacity, dtype=jnp.int32)
    send_onehot = ((send_slot[None, :] == slot_range[:, None]) & live_here[None, :]).astype(
        jnp.bfloat16
    )
    targets = seq_index * slot_count + jnp.arange(slot_count, dtype=jnp.int32)
    slot_match = (pack_dest[None, :, :] == targets[:, None, None]).astype(jnp.int32)
    block_range = jnp.arange(pack_dest.shape[1], dtype=jnp.int32)
    source_of = jnp.sum(slot_match * block_range[None, None, :], axis=(1, 2))
    request_of = jnp.sum(slot_match, axis=2)
    request_index = jnp.sum(request_of * jnp.arange(RQ, dtype=jnp.int32)[None, :], axis=1)
    pick_index = source_of * capacity + jnp.arange(slot_count, dtype=jnp.int32) % capacity
    owner_of = jnp.transpose(request_of) > 0
    local_rows, local_summary = compact_blocks(
        latent_cache, keep_onehot.astype(jnp.bfloat16), weights_dropped
    )
    send_rows = jnp.einsum(
        "jr,rkc->jkc", send_onehot, local_rows, preferred_element_type=jnp.float32
    )
    send_rows = send_rows.astype(jnp.bfloat16).reshape(seq_count, capacity, KB, row_width)
    send_summary = jnp.dot(send_onehot, local_summary, preferred_element_type=jnp.float32)
    send_summary = send_summary.astype(jnp.bfloat16).reshape(seq_count, capacity, row_width)
    recv_rows, recv_summary = (
        lax.all_to_all(send_rows, "seq", split_axis=0, concat_axis=0, tiled=True),
        lax.all_to_all(send_summary, "seq", split_axis=0, concat_axis=0, tiled=True),
    )
    packed_rows = jnp.take(
        recv_rows.reshape(seq_count * capacity, KB, row_width), pick_index, axis=0
    )
    packed_summary = jnp.take(
        recv_summary.reshape(seq_count * capacity, row_width), pick_index, axis=0
    )
    slot_query_lat = jnp.take(query_lat, request_index, axis=0)
    slot_query_rope = jnp.take(query_rope, request_index, axis=0)
    usable = jnp.ones((slot_count,), dtype=bool)
    maxima, totals, weighted = attend_blocks(
        slot_query_lat, slot_query_rope, packed_rows, packed_summary, usable
    )
    partial_value = per_request(maxima, totals, weighted, owner_of)
    request_max, request_total, request_sum = merged(partial_value, "seq", combine_partial)
    attended = (request_sum / request_total[:, :, None]).astype(jnp.bfloat16)
    values = jnp.einsum("rhl,hlv->rhv", attended, value_up, preferred_element_type=jnp.float32)
    values = values.astype(jnp.bfloat16).reshape(RQ, H * VH)
    col_width = out_weight.shape[1]
    residual = lax.dynamic_slice_in_dim(hidden_in, seq_index * col_width, col_width, 1)
    hidden_out = (
        residual.astype(jnp.float32)
        + jnp.dot(values, out_weight, preferred_element_type=jnp.float32)
    ).astype(jnp.bfloat16)
    gathered = lax.all_gather(hidden_out[None], ("seq", "mp"), axis=0, tiled=True)
    all_rows = gathered.reshape(seq_count, mp_count, RQ, col_width).transpose(1, 2, 0, 3)
    all_rows = all_rows.reshape(mp_count * RQ, seq_count * col_width)
    rows_f = all_rows.astype(jnp.float32)
    mean_sq = jnp.mean(rows_f * rows_f, axis=1)
    norms_all = jnp.sqrt(mean_sq)
    normed = (
        rows_f * lax.rsqrt(mean_sq + 1e-06)[:, None] * final_gain.astype(jnp.float32)[None, :]
    ).astype(jnp.bfloat16)
    logits = jnp.dot(normed, head_weight, preferred_element_type=jnp.float32)
    vocab_width = head_weight.shape[1]
    device_index = seq_index * mp_count + mp_index
    columns = device_index * vocab_width + jnp.arange(vocab_width, dtype=jnp.int32)
    tenant_onehot = (tenant_ids[:, None] == jnp.arange(TENANTS, dtype=jnp.int32)[None, :]).astype(
        jnp.int32
    )
    window_low = jnp.sum(tenant_onehot * tenant_ranges[None, :, 0], axis=1)
    window_high = jnp.sum(tenant_onehot * tenant_ranges[None, :, 1], axis=1)
    allowed = (columns[None, :] >= window_low[:, None]) & (columns[None, :] < window_high[:, None])
    local_best = jnp.max(jnp.where(allowed, logits, NEGATIVE), axis=1)
    best_all = lax.pmax(local_best, ("seq", "mp"))
    row_start = mp_index * RQ
    state_norm = lax.dynamic_slice_in_dim(norms_all, row_start, RQ, 0)
    top_logit = lax.dynamic_slice_in_dim(best_all, row_start, RQ, 0)
    return (packed_rows, packed_summary, hidden_out, state_norm, top_logit)


F32 = jnp.float32
BF16 = jnp.bfloat16
PAIR = 2 * RQ


def to_peer(src, dst, send_sem, recv_sem, device):
    copy = pltpu.make_async_remote_copy(
        src_ref=src,
        dst_ref=dst,
        send_sem=send_sem,
        recv_sem=recv_sem,
        device_id=device,
        device_id_type=pl.DeviceIdType.MESH,
    )
    copy.start()
    return copy


def as_row(column):
    wide = jnp.broadcast_to(column[:, :1], (RQ, RQ))
    sub = lax.broadcasted_iota(jnp.int32, (RQ, RQ), 0)
    lane = lax.broadcasted_iota(jnp.int32, (RQ, RQ), 1)
    return jnp.sum(jnp.where(sub == lane, wide, 0.0), axis=0, keepdims=True)


def unfold(part):
    wide = part.astype(F32)
    return jnp.concatenate([wide[:RQ], wide[RQ:]], axis=1)


def fold(x):
    width = x.shape[1] // 2
    return jnp.concatenate([x[:, :width], x[:, width:]], axis=0)


def layer_kernel(
    seq_count,
    mp_count,
    vocab_width,
    tile,
    hidden_ref,
    keep_ref,
    drop_ref,
    gain_ref,
    dest_ref,
    ranges_ref,
    ids_ref,
    query_hbm,
    absorb_hbm,
    up_hbm,
    out_hbm,
    cache_hbm,
    head_hbm,
    rows_out,
    summary_out,
    hidden_out,
    norm_out,
    top_out,
    query_w,
    absorb_w,
    up_w,
    out_w,
    cache,
    head_w,
    query_recv,
    query_flat,
    kept,
    summ,
    rows_send,
    rows_recv,
    summ_send,
    summ_recv,
    part_send,
    part_recv,
    value_recv,
    hidden_all,
    mp_best,
    mp_best_recv,
    seq_best,
    local_sem,
    q_send,
    q_recv,
    r_send,
    r_recv,
    s_send,
    s_recv,
    p_send,
    p_recv,
    v_send,
    v_recv,
    h_send,
    h_recv,
    g_send,
    g_recv,
    a_send,
    a_recv,
    b_send,
    b_recv,
):
    me = lax.axis_index("seq")
    my_mp = lax.axis_index("mp")
    slot_count = RQ // 2
    block_count = dest_ref.shape[1]
    row_width = LAT + ROPE
    head_width = NOPE + ROPE

    def seq_peer(k):
        return lax.rem(me + k, seq_count)

    def mp_peer(k):
        return lax.rem(my_mp + k, mp_count)

    def load(i, src, dst):
        copy = pltpu.make_async_copy(src, dst, local_sem.at[i])
        copy.start()
        return copy

    query_load = load(0, query_hbm, query_w)
    cache_load = load(1, cache_hbm, cache)
    absorb_load = load(2, absorb_hbm, absorb_w)

    barrier = pltpu.get_barrier_semaphore()
    for k in range(1, seq_count):
        pl.semaphore_signal(
            barrier, inc=1, device_id=(seq_peer(k), my_mp), device_id_type=pl.DeviceIdType.MESH
        )
    for k in range(1, mp_count):
        pl.semaphore_signal(
            barrier, inc=1, device_id=(me, mp_peer(k)), device_id_type=pl.DeviceIdType.MESH
        )

    keep = jnp.concatenate([keep_ref[:, 0, :], keep_ref[:, 0, :]], axis=1).astype(F32)
    keep_t = jnp.transpose(keep)[:KB]
    position = lax.broadcasted_iota(jnp.int32, (KB, BLK), 1).astype(F32)
    request_sub = lax.broadcasted_iota(jnp.int32, (RQ, BLK), 0)
    picks = []
    kept_flag = jnp.zeros((RQ, BLK), F32)
    for r in range(RQ):
        pick = jnp.where(jnp.broadcast_to(keep_t[:, r : r + 1], (KB, BLK)) == position, 1.0, 0.0)
        flag = jnp.sum(pick, axis=0, keepdims=True)
        kept_flag = jnp.where(request_sub == r, jnp.broadcast_to(flag, (RQ, BLK)), kept_flag)
        picks.append(pick.astype(BF16))
    dropped = drop_ref[...].astype(F32) * (1.0 - kept_flag)
    mass = jnp.sum(dropped, axis=1, keepdims=True)

    query_load.wait()
    query = jnp.dot(hidden_ref[...], query_w[...], preferred_element_type=F32)
    query_recv[me] = fold(query).astype(BF16)
    pl.semaphore_wait(barrier, seq_count + mp_count - 2)
    sends = []
    query_copies = [
        to_peer(
            query_recv.at[me],
            query_recv.at[me],
            q_send.at[k - 1],
            q_recv.at[k - 1],
            (seq_peer(k), my_mp),
        )
        for k in range(1, seq_count)
    ]
    out_load = load(3, out_hbm, out_w)
    up_load = load(4, up_hbm.at[pl.ds(me * 2, 2)], up_w)
    head_load = load(5, head_hbm, head_w)

    cache_load.wait()
    summed = jnp.zeros((PAIR, row_width), F32)
    pad = jnp.zeros((PAIR - RQ, BLK), F32)
    for r in range(RQ):
        kept[r] = jnp.dot(picks[r], cache[r], preferred_element_type=F32).astype(BF16)
        own = jnp.where(request_sub == r, dropped, 0.0)
        own = jnp.concatenate([own, pad], axis=0).astype(BF16)
        summed = summed + jnp.dot(own, cache[r], preferred_element_type=F32)
    mass_pair = jnp.concatenate([mass, jnp.ones_like(mass)], axis=0)
    summary = (summed / mass_pair).astype(BF16)
    summ[...] = summary
    summary_f = summary.astype(F32)[:RQ]
    low_part = summary_f[:, :384]
    high_part = jnp.concatenate([summary_f[:, 384:], jnp.zeros((RQ, 768 - row_width), F32)], axis=1)
    folded_summary = jnp.concatenate([low_part, high_part], axis=0).astype(BF16)
    summ_send[...] = folded_summary
    summ_recv[me] = folded_summary

    owners = [dest_ref[r, me] >> 2 for r in range(RQ)]

    def request_for(owner):
        chosen = jnp.int32(0)
        for r in range(RQ):
            chosen = jnp.where(owners[r] == owner, jnp.int32(r), chosen)
        return chosen

    rows_recv[me] = kept[request_for(me)]
    for k in range(1, seq_count):
        rows_send[k - 1] = kept[request_for(seq_peer(k))]

    def start_pack():
        started = []
        for k in range(1, seq_count):
            started.append(
                to_peer(
                    summ_send,
                    summ_recv.at[me],
                    s_send.at[k - 1],
                    s_recv.at[k - 1],
                    (seq_peer(k), my_mp),
                )
            )
            started.append(
                to_peer(
                    rows_send.at[k - 1],
                    rows_recv.at[me],
                    r_send.at[k - 1],
                    r_recv.at[k - 1],
                    (seq_peer(k), my_mp),
                )
            )
        return started

    pack_copies = start_pack()

    absorb_load.wait()
    for copy in query_copies:
        copy.wait_recv()
    first_half = lax.broadcasted_iota(jnp.int32, (PAIR, NOPE), 0) < RQ
    for s in range(seq_count):
        part = query_recv[s]
        nope = part[:, :NOPE].astype(F32)
        split = jnp.concatenate(
            [jnp.where(first_half, nope, 0.0), jnp.where(first_half, 0.0, nope)], axis=1
        ).astype(BF16)
        weight = absorb_w[2 * s : 2 * s + 2].reshape(2 * NOPE, LAT)
        latent = jnp.dot(split, weight, preferred_element_type=F32).astype(BF16)
        query_flat[PAIR * s : PAIR * (s + 1), :LAT] = latent
        query_flat[PAIR * s : PAIR * (s + 1), LAT:] = part[:, NOPE:]

    rows = H * RQ
    score_scale = (NOPE + ROPE) ** (-0.5)
    contract = (((1,), (1,)), ((), ()))
    flat = query_flat[...]
    kept_all = kept[...].reshape(RQ * KB, row_width)
    row_scores = lax.dot_general(flat, kept_all, contract, preferred_element_type=F32)
    summ_scores = lax.dot_general(flat, summ[...], contract, preferred_element_type=F32)
    row_request = lax.broadcasted_iota(jnp.int32, (rows, RQ * KB), 0) & (RQ - 1)
    col_request = lax.broadcasted_iota(jnp.int32, (rows, RQ * KB), 1) // KB
    row_scores = jnp.where(row_request == col_request, row_scores * score_scale, NEGATIVE)
    summ_request = lax.broadcasted_iota(jnp.int32, (rows, PAIR), 0) & (RQ - 1)
    summ_column = lax.broadcasted_iota(jnp.int32, (rows, PAIR), 1)
    summ_scores = summ_scores * score_scale + jnp.log(F32(BLK - KB))
    summ_scores = jnp.where(summ_request == summ_column, summ_scores, NEGATIVE)
    maxima = jnp.maximum(
        jnp.max(row_scores, axis=1, keepdims=True), jnp.max(summ_scores, axis=1, keepdims=True)
    )
    row_weights = jnp.exp(row_scores - maxima)
    summ_weights = jnp.exp(summ_scores - maxima)
    totals = jnp.sum(row_weights, axis=1, keepdims=True) + jnp.sum(
        summ_weights, axis=1, keepdims=True
    )
    weighted = jnp.dot(
        row_weights.astype(BF16), kept_all[:, :LAT], preferred_element_type=F32
    ) + jnp.dot(summ_weights.astype(BF16), summ[:, :LAT], preferred_element_type=F32)
    live_rows = lax.broadcasted_iota(jnp.int32, (rows, 128), 0) & (RQ - 1)
    level = jnp.broadcast_to(maxima + jnp.log(totals), (rows, 128))
    for r in range(RQ):
        level = jnp.where((live_rows == r) & (owners[r] < 0), NEGATIVE, level)
    high = level.astype(BF16).astype(F32)
    middle = (level - high).astype(BF16).astype(F32)
    low = level - high - middle
    lane = lax.broadcasted_iota(jnp.int32, (rows, 128), 1)
    terms = jnp.where(
        lane == 0, high, jnp.where(lane == 1, middle, jnp.where(lane == 2, low, 0.0))
    )
    part_send[:, :, :LAT] = (weighted / totals).astype(BF16).reshape(seq_count, PAIR, LAT)
    part_send[:, :, LAT:] = terms.astype(BF16).reshape(seq_count, PAIR, 128)
    part_copies = [
        to_peer(
            part_send.at[seq_peer(k)],
            part_recv.at[me],
            p_send.at[k - 1],
            p_recv.at[k - 1],
            (seq_peer(k), my_mp),
        )
        for k in range(1, seq_count)
    ]
    part_recv[me] = part_send[me]

    total_rows = mp_count * RQ
    window_row = lax.broadcasted_iota(jnp.int32, (total_rows, 128), 0)
    window_low = jnp.zeros((total_rows, 128), jnp.int32)
    window_high = jnp.zeros((total_rows, 128), jnp.int32)
    for row in range(total_rows):
        tenant = ids_ref[row]
        window_low = jnp.where(window_row == row, ranges_ref[tenant, 0], window_low)
        window_high = jnp.where(window_row == row, ranges_ref[tenant, 1], window_high)
    vocab_start = (me * mp_count + my_mp) * vocab_width
    window_low = window_low - vocab_start
    window_high = window_high - vocab_start

    slot_code = [jnp.int32(0)] * slot_count
    for r in range(RQ):
        for b in range(block_count):
            offset = dest_ref[r, b] - me * slot_count
            for j in range(slot_count):
                slot_code[j] = jnp.where(offset == j, jnp.int32(b * RQ + r), slot_code[j])

    up_load.wait()
    for copy in part_copies:
        copy.wait_recv()
    levels = [
        jnp.sum(part_recv[s, :, LAT:].astype(F32), axis=1, keepdims=True)
        for s in range(seq_count)
    ]
    peak = functools.reduce(jnp.maximum, levels)
    factors = [jnp.exp(part_level - peak) for part_level in levels]
    merged_sum = functools.reduce(
        jnp.add, [factors[s] * part_recv[s, :, :LAT].astype(F32) for s in range(seq_count)]
    )
    attended = (merged_sum / functools.reduce(jnp.add, factors)).astype(BF16).astype(F32)
    first_wide = lax.broadcasted_iota(jnp.int32, (PAIR, LAT), 0) < RQ
    split = jnp.concatenate(
        [jnp.where(first_wide, attended, 0.0), jnp.where(first_wide, 0.0, attended)], axis=1
    ).astype(BF16)
    values = jnp.dot(split, up_w[...].reshape(2 * LAT, VH), preferred_element_type=F32)
    value_recv[me] = values.astype(BF16)
    value_copies = [
        to_peer(
            value_recv.at[me],
            value_recv.at[me],
            v_send.at[k - 1],
            v_recv.at[k - 1],
            (seq_peer(k), my_mp),
        )
        for k in range(1, seq_count)
    ]
    out_load.wait()
    for copy in value_copies:
        copy.wait_recv()
    all_values = jnp.concatenate(
        [unfold(value_recv[s]) for s in range(seq_count)], axis=1
    ).astype(BF16)
    col_width = out_w.shape[1]
    residual = hidden_ref[:, pl.ds(pl.multiple_of(me * col_width, 128), col_width)]
    hidden = residual.astype(F32) + jnp.dot(all_values, out_w[...], preferred_element_type=F32)
    hidden = hidden.astype(BF16)
    hidden_out[...] = hidden
    hidden_all[my_mp, me] = fold(hidden.astype(F32)).astype(BF16)

    hidden_copies = [
        to_peer(
            hidden_all.at[my_mp, me],
            hidden_all.at[my_mp, me],
            h_send.at[k - 1],
            h_recv.at[k - 1],
            (seq_peer(k), my_mp),
        )
        for k in range(1, seq_count)
    ]
    for copy in hidden_copies:
        copy.wait_recv()
    group_copies = [
        to_peer(
            hidden_all.at[my_mp],
            hidden_all.at[my_mp],
            g_send.at[k - 1],
            g_recv.at[k - 1],
            (me, mp_peer(k)),
        )
        for k in range(1, mp_count)
    ]
    own_rows = jnp.concatenate(
        [unfold(hidden_all[my_mp, s]) for s in range(seq_count)], axis=1
    )
    own_norm = jnp.sqrt(jnp.mean(own_rows * own_rows, axis=1, keepdims=True))
    norm_out[...] = as_row(own_norm)
    gain = gain_ref[...].astype(F32)
    for copy in group_copies:
        copy.wait_recv()
    normed = []
    for m in range(mp_count):
        group = jnp.concatenate([unfold(hidden_all[m, s]) for s in range(seq_count)], axis=1)
        mean_sq = jnp.mean(group * group, axis=1, keepdims=True)
        normed.append(group * lax.rsqrt(mean_sq + 1e-06) * gain)
    normed = jnp.concatenate(normed, axis=0).astype(BF16)

    head_load.wait()
    lane = lax.broadcasted_iota(jnp.int32, (total_rows, 128), 1)

    def head_step(n, best):
        start = pl.multiple_of(n * tile, 128)
        logits = jnp.dot(normed, head_w[:, pl.ds(start, tile)], preferred_element_type=F32)
        for i in range(tile // 128):
            column = lane + (start + i * 128)
            allowed = (column >= window_low) & (column < window_high)
            best = jnp.maximum(
                best, jnp.where(allowed, logits[:, i * 128 : (i + 1) * 128], NEGATIVE)
            )
        return best

    best = lax.fori_loop(
        0, vocab_width // tile, head_step, jnp.full((total_rows, 128), NEGATIVE, F32)
    )
    best = jnp.broadcast_to(jnp.max(best, axis=1, keepdims=True), (total_rows, 128))
    mp_best[...] = best.reshape(mp_count, RQ, 128)
    mp_best_recv[my_mp] = mp_best[my_mp]
    best_copies = [
        to_peer(
            mp_best.at[mp_peer(k)],
            mp_best_recv.at[my_mp],
            a_send.at[k - 1],
            a_recv.at[k - 1],
            (me, mp_peer(k)),
        )
        for k in range(1, mp_count)
    ]
    for copy in best_copies:
        copy.wait_recv()
    seq_best[me] = jnp.max(mp_best_recv[...], axis=0)
    last_copies = [
        to_peer(
            seq_best.at[me],
            seq_best.at[me],
            b_send.at[k - 1],
            b_recv.at[k - 1],
            (seq_peer(k), my_mp),
        )
        for k in range(1, seq_count)
    ]

    for copy in pack_copies:
        copy.wait_recv()
    half_sub = lax.broadcasted_iota(jnp.int32, (PAIR, 384), 0)
    for j in range(slot_count):
        source = slot_code[j] // RQ
        request = slot_code[j] % RQ
        rows_out[j] = rows_recv[source]
        both = summ_recv[source].astype(F32)
        low_row = jnp.sum(jnp.where(half_sub == request, both, 0.0), axis=0, keepdims=True)
        high_row = jnp.sum(jnp.where(half_sub == request + RQ, both, 0.0), axis=0, keepdims=True)
        line = jnp.concatenate([low_row, high_row[:, : row_width - 384]], axis=1)
        summary_out[j : j + 1, :] = line

    for copy in last_copies:
        copy.wait_recv()
    top_out[...] = as_row(jnp.max(seq_best[...], axis=0))
    for copy in (
        query_copies
        + pack_copies
        + part_copies
        + value_copies
        + hidden_copies
        + group_copies
        + best_copies
        + last_copies
    ):
        copy.wait_send()


def fused_body(
    hidden_in,
    query_weight,
    key_absorb,
    value_up,
    out_weight,
    latent_cache,
    cache_lengths,
    keep_lists,
    drop_weights,
    pack_dest,
    final_gain,
    head_weight,
    tenant_ranges,
    tenant_ids,
):
    seq_count = lax.axis_size("seq")
    mp_count = lax.axis_size("mp")
    row_width = LAT + ROPE
    slot_count = RQ // 2
    depth, vocab_width = head_weight.shape
    tile = next(t for t in (640, 512, 384, 256, 128) if vocab_width % t == 0)
    vmem = pl.BlockSpec(memory_space=pltpu.VMEM)
    smem = pl.BlockSpec(memory_space=pltpu.SMEM)
    hbm = pl.BlockSpec(memory_space=pl.ANY)
    seq_sems = pltpu.SemaphoreType.DMA((seq_count - 1,))
    mp_sems = pltpu.SemaphoreType.DMA((mp_count - 1,))
    outs = pl.pallas_call(
        functools.partial(layer_kernel, seq_count, mp_count, vocab_width, tile),
        out_shape=(
            jax.ShapeDtypeStruct((slot_count, KB, row_width), BF16),
            jax.ShapeDtypeStruct((slot_count, row_width), F32),
            jax.ShapeDtypeStruct((RQ, out_weight.shape[1]), BF16),
            jax.ShapeDtypeStruct((1, RQ), F32),
            jax.ShapeDtypeStruct((1, RQ), F32),
        ),
        in_specs=[vmem] * 4 + [smem] * 3 + [hbm] * 6,
        out_specs=(vmem,) * 5,
        scratch_shapes=[
            pltpu.VMEM(query_weight.shape, BF16),
            pltpu.VMEM(key_absorb.shape, BF16),
            pltpu.VMEM((2,) + value_up.shape[1:], BF16),
            pltpu.VMEM(out_weight.shape, BF16),
            pltpu.VMEM(latent_cache.shape, BF16),
            pltpu.VMEM(head_weight.shape, BF16),
            pltpu.VMEM((seq_count, PAIR, NOPE + ROPE), BF16),
            pltpu.VMEM((H * RQ, row_width), BF16),
            pltpu.VMEM((RQ, KB, row_width), BF16),
            pltpu.VMEM((PAIR, row_width), BF16),
            pltpu.VMEM((seq_count - 1, KB, row_width), BF16),
            pltpu.VMEM((seq_count, KB, row_width), BF16),
            pltpu.VMEM((PAIR, 384), BF16),
            pltpu.VMEM((seq_count, PAIR, 384), BF16),
            pltpu.VMEM((seq_count, PAIR, LAT + 128), BF16),
            pltpu.VMEM((seq_count, PAIR, LAT + 128), BF16),
            pltpu.VMEM((seq_count, PAIR, VH), BF16),
            pltpu.VMEM((mp_count, seq_count, PAIR, out_weight.shape[1] // 2), BF16),
            pltpu.VMEM((mp_count, RQ, 128), F32),
            pltpu.VMEM((mp_count, RQ, 128), F32),
            pltpu.VMEM((seq_count, RQ, 128), F32),
            pltpu.SemaphoreType.DMA((6,)),
        ]
        + [seq_sems] * 12
        + [mp_sems] * 4
        + [seq_sems] * 2,
        compiler_params=pltpu.CompilerParams(
            collective_id=0, has_side_effects=True, vmem_limit_bytes=48 * 2**20
        ),
    )(
        hidden_in,
        keep_lists,
        drop_weights,
        final_gain.reshape(1, -1),
        pack_dest,
        tenant_ranges,
        tenant_ids,
        query_weight,
        key_absorb,
        value_up,
        out_weight,
        latent_cache,
        head_weight,
    )
    packed_rows, packed_summary, hidden_out, state_norm, top_logit = outs
    return (
        packed_rows,
        packed_summary.astype(BF16),
        hidden_out,
        state_norm.reshape(RQ),
        top_logit.reshape(RQ),
    )


def solution(mesh):
    in_specs = (
        P("mp", None),
        P(None, "seq"),
        P(),
        P(),
        P(None, "seq"),
        P("mp", "seq", None),
        P("mp"),
        P("mp", "seq", None),
        P("mp", "seq"),
        P("mp", None),
        P(),
        P(None, ("seq", "mp")),
        P(),
        P(),
    )
    out_specs = (
        P(("seq", "mp"), None, None),
        P(("seq", "mp"), None),
        P("mp", "seq"),
        P("mp"),
        P("mp"),
    )
    seq_count = mesh.shape["seq"]
    fused = seq_count * 2 == H
    return jax.shard_map(fused_body if fused else body, mesh=mesh, in_specs=in_specs, out_specs=out_specs, check_vma=False)
```

```python
import functools

import jax
import jax.numpy as jnp
from jax import lax
from jax.experimental import pallas as pl
from jax.experimental.pallas import tpu as pltpu
from jax.sharding import PartitionSpec as P

H = 16
NOPE = 128
ROPE = 64
LAT = 512
VH = 128
BLK = 128
KB = 64
TENANTS = 4
RQ = 8


NEGATIVE = -1e30
HIGHEST = lax.Precision.HIGHEST


def merged(x, axis, combine):
    everything = jax.tree.map(lambda part: lax.all_gather(part, axis), x)
    initial = jax.tree.map(lambda part: part[0], everything)

    def step(k, so_far):
        return combine(so_far, jax.tree.map(lambda part: part[k], everything))

    return lax.fori_loop(1, lax.axis_size(axis), step, initial)


def compact_blocks(block_rows, keep_onehot, weights_dropped):
    kept_rows = jnp.einsum(
        "nkt,ntc->nkc", keep_onehot, block_rows, preferred_element_type=jnp.float32
    ).astype(jnp.bfloat16)
    weight_mass = jnp.sum(weights_dropped.astype(jnp.float32), axis=1)
    summed = jnp.einsum(
        "nt,ntc->nc", weights_dropped, block_rows, preferred_element_type=jnp.float32
    )
    summary = (summed / weight_mass[:, None]).astype(jnp.bfloat16)
    return (kept_rows, summary)


def attend_blocks(query_lat, query_rope, kept_rows, summary, usable):
    score_scale = (NOPE + ROPE) ** (-0.5)
    row_scores = (
        jnp.einsum(
            "nhl,nkl->nhk", query_lat, kept_rows[:, :, :LAT], preferred_element_type=jnp.float32
        )
        + jnp.einsum(
            "nhr,nkr->nhk", query_rope, kept_rows[:, :, LAT:], preferred_element_type=jnp.float32
        )
    ) * score_scale
    summ_scores = (
        jnp.einsum("nhl,nl->nh", query_lat, summary[:, :LAT], preferred_element_type=jnp.float32)
        + jnp.einsum("nhr,nr->nh", query_rope, summary[:, LAT:], preferred_element_type=jnp.float32)
    ) * score_scale
    summ_scores = summ_scores + jnp.log(jnp.float32(BLK - KB))
    row_scores = jnp.where(usable[:, None, None], row_scores, NEGATIVE)
    summ_scores = jnp.where(usable[:, None], summ_scores, NEGATIVE)
    maxima = jnp.maximum(jnp.max(row_scores, axis=2), summ_scores)
    row_weights = jnp.where(usable[:, None, None], jnp.exp(row_scores - maxima[:, :, None]), 0.0)
    summ_weights = jnp.where(usable[:, None], jnp.exp(summ_scores - maxima), 0.0)
    totals = jnp.sum(row_weights, axis=2) + summ_weights
    weighted = jnp.einsum(
        "nhk,nkl->nhl", row_weights, kept_rows[:, :, :LAT].astype(jnp.float32), precision=HIGHEST
    )
    weighted = weighted + summ_weights[:, :, None] * summary[:, None, :LAT].astype(jnp.float32)
    return (maxima, totals, weighted)


def per_request(maxima, totals, weighted, owner_of):
    request_max = jnp.max(jnp.where(owner_of[:, :, None], maxima[None, :, :], NEGATIVE), axis=1)
    shifted = jnp.where(owner_of[:, :, None], maxima[None, :, :] - request_max[:, None, :], 0.0)
    factor = jnp.where(owner_of[:, :, None], jnp.exp(shifted), 0.0)
    request_total = jnp.einsum("rnh,nh->rh", factor, totals, precision=HIGHEST)
    request_sum = jnp.einsum("rnh,nhl->rhl", factor, weighted, precision=HIGHEST)
    return (request_max, request_total, request_sum)


def combine_partial(former, latter):
    former_max, former_total, former_sum = former
    latter_max, latter_total, latter_sum = latter
    joined = jnp.maximum(former_max, latter_max)
    former_factor = jnp.exp(former_max - joined)
    latter_factor = jnp.exp(latter_max - joined)
    return (
        joined,
        former_factor * former_total + latter_factor * latter_total,
        former_factor[:, :, None] * former_sum + latter_factor[:, :, None] * latter_sum,
    )


def body(
    hidden_in,
    query_weight,
    key_absorb,
    value_up,
    out_weight,
    latent_cache,
    cache_lengths,
    keep_lists,
    drop_weights,
    pack_dest,
    final_gain,
    head_weight,
    tenant_ranges,
    tenant_ids,
):
    seq_count = lax.axis_size("seq")
    mp_count = lax.axis_size("mp")
    seq_index = lax.axis_index("seq")
    mp_index = lax.axis_index("mp")
    capacity = max(1, RQ // seq_count)
    slot_count = RQ // 2
    row_width = LAT + ROPE
    query_part = jnp.dot(hidden_in, query_weight, preferred_element_type=jnp.float32).astype(
        jnp.bfloat16
    )
    query_full = lax.all_gather(query_part, "seq", axis=1, tiled=True).reshape(RQ, H, NOPE + ROPE)
    query_lat = jnp.einsum(
        "rhn,hnl->rhl", query_full[:, :, :NOPE], key_absorb, preferred_element_type=jnp.float32
    ).astype(jnp.bfloat16)
    query_rope = query_full[:, :, NOPE:]
    positions = jnp.arange(BLK, dtype=jnp.int32)
    keep_onehot = keep_lists[:, 0, :, None] == positions[None, None, :]
    kept_flag = jnp.sum(keep_onehot.astype(jnp.int32), axis=1)
    weights_dropped = (drop_weights * (1 - kept_flag)).astype(jnp.bfloat16)
    live_here = cache_lengths > seq_index * BLK
    dest_here = lax.dynamic_slice_in_dim(pack_dest, seq_index, 1, 1)[:, 0]
    send_slot = dest_here // slot_count * capacity + dest_here % slot_count % capacity
    slot_range = jnp.arange(seq_count * capacity, dtype=jnp.int32)
    send_onehot = ((send_slot[None, :] == slot_range[:, None]) & live_here[None, :]).astype(
        jnp.bfloat16
    )
    targets = seq_index * slot_count + jnp.arange(slot_count, dtype=jnp.int32)
    slot_match = (pack_dest[None, :, :] == targets[:, None, None]).astype(jnp.int32)
    block_range = jnp.arange(pack_dest.shape[1], dtype=jnp.int32)
    source_of = jnp.sum(slot_match * block_range[None, None, :], axis=(1, 2))
    request_of = jnp.sum(slot_match, axis=2)
    request_index = jnp.sum(request_of * jnp.arange(RQ, dtype=jnp.int32)[None, :], axis=1)
    pick_index = source_of * capacity + jnp.arange(slot_count, dtype=jnp.int32) % capacity
    owner_of = jnp.transpose(request_of) > 0
    local_rows, local_summary = compact_blocks(
        latent_cache, keep_onehot.astype(jnp.bfloat16), weights_dropped
    )
    send_rows = jnp.einsum(
        "jr,rkc->jkc", send_onehot, local_rows, preferred_element_type=jnp.float32
    )
    send_rows = send_rows.astype(jnp.bfloat16).reshape(seq_count, capacity, KB, row_width)
    send_summary = jnp.dot(send_onehot, local_summary, preferred_element_type=jnp.float32)
    send_summary = send_summary.astype(jnp.bfloat16).reshape(seq_count, capacity, row_width)
    recv_rows, recv_summary = (
        lax.all_to_all(send_rows, "seq", split_axis=0, concat_axis=0, tiled=True),
        lax.all_to_all(send_summary, "seq", split_axis=0, concat_axis=0, tiled=True),
    )
    packed_rows = jnp.take(
        recv_rows.reshape(seq_count * capacity, KB, row_width), pick_index, axis=0
    )
    packed_summary = jnp.take(
        recv_summary.reshape(seq_count * capacity, row_width), pick_index, axis=0
    )
    slot_query_lat = jnp.take(query_lat, request_index, axis=0)
    slot_query_rope = jnp.take(query_rope, request_index, axis=0)
    usable = jnp.ones((slot_count,), dtype=bool)
    maxima, totals, weighted = attend_blocks(
        slot_query_lat, slot_query_rope, packed_rows, packed_summary, usable
    )
    partial_value = per_request(maxima, totals, weighted, owner_of)
    request_max, request_total, request_sum = merged(partial_value, "seq", combine_partial)
    attended = (request_sum / request_total[:, :, None]).astype(jnp.bfloat16)
    values = jnp.einsum("rhl,hlv->rhv", attended, value_up, preferred_element_type=jnp.float32)
    values = values.astype(jnp.bfloat16).reshape(RQ, H * VH)
    col_width = out_weight.shape[1]
    residual = lax.dynamic_slice_in_dim(hidden_in, seq_index * col_width, col_width, 1)
    hidden_out = (
        residual.astype(jnp.float32)
        + jnp.dot(values, out_weight, preferred_element_type=jnp.float32)
    ).astype(jnp.bfloat16)
    gathered = lax.all_gather(hidden_out[None], ("seq", "mp"), axis=0, tiled=True)
    all_rows = gathered.reshape(seq_count, mp_count, RQ, col_width).transpose(1, 2, 0, 3)
    all_rows = all_rows.reshape(mp_count * RQ, seq_count * col_width)
    rows_f = all_rows.astype(jnp.float32)
    mean_sq = jnp.mean(rows_f * rows_f, axis=1)
    norms_all = jnp.sqrt(mean_sq)
    normed = (
        rows_f * lax.rsqrt(mean_sq + 1e-06)[:, None] * final_gain.astype(jnp.float32)[None, :]
    ).astype(jnp.bfloat16)
    logits = jnp.dot(normed, head_weight, preferred_element_type=jnp.float32)
    vocab_width = head_weight.shape[1]
    device_index = seq_index * mp_count + mp_index
    columns = device_index * vocab_width + jnp.arange(vocab_width, dtype=jnp.int32)
    tenant_onehot = (tenant_ids[:, None] == jnp.arange(TENANTS, dtype=jnp.int32)[None, :]).astype(
        jnp.int32
    )
    window_low = jnp.sum(tenant_onehot * tenant_ranges[None, :, 0], axis=1)
    window_high = jnp.sum(tenant_onehot * tenant_ranges[None, :, 1], axis=1)
    allowed = (columns[None, :] >= window_low[:, None]) & (columns[None, :] < window_high[:, None])
    local_best = jnp.max(jnp.where(allowed, logits, NEGATIVE), axis=1)
    best_all = lax.pmax(local_best, ("seq", "mp"))
    row_start = mp_index * RQ
    state_norm = lax.dynamic_slice_in_dim(norms_all, row_start, RQ, 0)
    top_logit = lax.dynamic_slice_in_dim(best_all, row_start, RQ, 0)
    return (packed_rows, packed_summary, hidden_out, state_norm, top_logit)


F32 = jnp.float32
BF16 = jnp.bfloat16
PAIR = 2 * RQ
LANES = 128
ROPE_AT = LAT // LANES * KB
SUMM_AT = ROPE_AT + KB // 2
MESSAGE = SUMM_AT + PAIR


def to_peer(src, dst, send_sem, recv_sem, device):
    copy = pltpu.make_async_remote_copy(
        src_ref=src,
        dst_ref=dst,
        send_sem=send_sem,
        recv_sem=recv_sem,
        device_id=device,
        device_id_type=pl.DeviceIdType.MESH,
    )
    copy.start()
    return copy


def as_row(column):
    wide = jnp.broadcast_to(column[:, :1], (RQ, RQ))
    sub = lax.broadcasted_iota(jnp.int32, (RQ, RQ), 0)
    lane = lax.broadcasted_iota(jnp.int32, (RQ, RQ), 1)
    return jnp.sum(jnp.where(sub == lane, wide, 0.0), axis=0, keepdims=True)


def unfold(part):
    wide = part.astype(F32)
    return jnp.concatenate([wide[:RQ], wide[RQ:]], axis=1)


def fold(x):
    width = x.shape[1] // 2
    return jnp.concatenate([x[:, :width], x[:, width:]], axis=0)


def layer_kernel(
    seq_count,
    mp_count,
    vocab_width,
    tile,
    hidden_ref,
    keep_ref,
    drop_ref,
    gain_ref,
    dest_ref,
    ranges_ref,
    ids_ref,
    query_hbm,
    absorb_hbm,
    up_hbm,
    out_hbm,
    cache_hbm,
    head_hbm,
    rows_out,
    summary_out,
    hidden_out,
    norm_out,
    top_out,
    query_w,
    absorb_w,
    up_w,
    out_w,
    cache,
    head_w,
    query_recv,
    query_flat,
    kept,
    summ,
    blocks,
    block_send,
    block_recv,
    part_send,
    part_recv,
    value_recv,
    hidden_all,
    mp_best,
    mp_best_recv,
    seq_best,
    local_sem,
    q_send,
    q_recv,
    r_send,
    r_recv,
    p_send,
    p_recv,
    v_send,
    v_recv,
    h_send,
    h_recv,
    g_send,
    g_recv,
    a_send,
    a_recv,
    b_send,
    b_recv,
):
    me = lax.axis_index("seq")
    my_mp = lax.axis_index("mp")
    slot_count = RQ // 2
    block_count = dest_ref.shape[1]
    row_width = LAT + ROPE
    contract = (((1,), (1,)), ((), ()))

    def seq_peer(k):
        return lax.rem(me + k, seq_count)

    def mp_peer(k):
        return lax.rem(my_mp + k, mp_count)

    def load(i, src, dst):
        copy = pltpu.make_async_copy(src, dst, local_sem.at[i])
        copy.start()
        return copy

    query_load = load(0, query_hbm, query_w)
    cache_load = load(1, cache_hbm, cache)
    absorb_load = load(2, absorb_hbm, absorb_w)

    barrier = pltpu.get_barrier_semaphore()
    for k in range(1, seq_count):
        pl.semaphore_signal(
            barrier, inc=1, device_id=(seq_peer(k), my_mp), device_id_type=pl.DeviceIdType.MESH
        )
    for k in range(1, mp_count):
        pl.semaphore_signal(
            barrier, inc=1, device_id=(me, mp_peer(k)), device_id_type=pl.DeviceIdType.MESH
        )

    keep = jnp.concatenate([keep_ref[:, 0, :], keep_ref[:, 0, :]], axis=1).astype(F32)
    keep_t = jnp.transpose(keep)[:KB]
    position = lax.broadcasted_iota(jnp.int32, (KB, BLK), 1).astype(F32)
    request_sub = lax.broadcasted_iota(jnp.int32, (RQ, BLK), 0)
    picks = []
    kept_flag = jnp.zeros((RQ, BLK), F32)
    for r in range(RQ):
        pick = jnp.where(jnp.broadcast_to(keep_t[:, r : r + 1], (KB, BLK)) == position, 1.0, 0.0)
        flag = jnp.sum(pick, axis=0, keepdims=True)
        kept_flag = jnp.where(request_sub == r, jnp.broadcast_to(flag, (RQ, BLK)), kept_flag)
        picks.append(pick.astype(BF16))
    dropped = drop_ref[...].astype(F32) * (1.0 - kept_flag)
    mass = jnp.sum(dropped, axis=1, keepdims=True)

    query_load.wait()
    query = jnp.dot(hidden_ref[...], query_w[...], preferred_element_type=F32)
    query_recv[me] = fold(query).astype(BF16)
    pl.semaphore_wait(barrier, seq_count + mp_count - 2)
    query_copies = [
        to_peer(
            query_recv.at[me],
            query_recv.at[me],
            q_send.at[k - 1],
            q_recv.at[k - 1],
            (seq_peer(k), my_mp),
        )
        for k in range(1, seq_count)
    ]
    out_load = load(3, out_hbm, out_w)
    up_load = load(4, up_hbm.at[pl.ds(me * 2, 2)], up_w)
    head_load = load(5, head_hbm, head_w)

    cache_load.wait()
    summed = jnp.zeros((PAIR, row_width), F32)
    pad = jnp.zeros((PAIR - RQ, BLK), F32)
    for r in range(RQ):
        chosen = lax.dot_general(picks[r], cache[r], contract, preferred_element_type=F32)
        kept[r] = chosen.astype(BF16)
        for i in range(LAT // LANES):
            piece = chosen[:, i * LANES : (i + 1) * LANES]
            blocks[r, i * KB : (i + 1) * KB, :] = piece.astype(BF16)
        rope = chosen[:, LAT:]
        rope = jnp.concatenate([rope[: KB // 2], rope[KB // 2 :]], axis=1)
        blocks[r, ROPE_AT:SUMM_AT, :] = rope.astype(BF16)
        own = jnp.where(request_sub == r, dropped, 0.0)
        own = jnp.concatenate([own, pad], axis=0).astype(BF16)
        summed = summed + lax.dot_general(own, cache[r], contract, preferred_element_type=F32)
    mass_pair = jnp.concatenate([mass, jnp.ones_like(mass)], axis=0)
    summary = (summed / mass_pair).astype(BF16)
    summ[...] = summary
    summary_f = summary.astype(F32)[:RQ]
    summary_f = jnp.concatenate(
        [summary_f, jnp.zeros((RQ, 5 * LANES - row_width), F32)], axis=1
    )
    line = lax.broadcasted_iota(jnp.int32, (PAIR, LANES), 0)
    for r in range(RQ):
        lines = jnp.zeros((PAIR, LANES), F32)
        for i in range(5):
            piece = summary_f[r : r + 1, i * LANES : (i + 1) * LANES]
            lines = jnp.where(line == i, jnp.broadcast_to(piece, (PAIR, LANES)), lines)
        blocks[r, SUMM_AT:, :] = lines.astype(BF16)

    owners = [dest_ref[r, me] >> 2 for r in range(RQ)]

    def request_for(owner):
        chosen = jnp.int32(0)
        for r in range(RQ):
            chosen = jnp.where(owners[r] == owner, jnp.int32(r), chosen)
        return chosen

    block_recv[me] = blocks[request_for(me)]
    for k in range(1, seq_count):
        block_send[k - 1] = blocks[request_for(seq_peer(k))]

    def start_pack(k):
        return to_peer(
            block_send.at[k - 1],
            block_recv.at[me],
            r_send.at[k - 1],
            r_recv.at[k - 1],
            (seq_peer(k), my_mp),
        )

    absorb_load.wait()
    for copy in query_copies:
        copy.wait_recv()
    first_half = lax.broadcasted_iota(jnp.int32, (PAIR, NOPE), 0) < RQ
    for s in range(seq_count):
        part = query_recv[s]
        nope = part[:, :NOPE].astype(F32)
        split = jnp.concatenate(
            [jnp.where(first_half, nope, 0.0), jnp.where(first_half, 0.0, nope)], axis=1
        ).astype(BF16)
        weight = absorb_w[2 * s : 2 * s + 2].reshape(2 * NOPE, LAT)
        latent = jnp.dot(split, weight, preferred_element_type=F32).astype(BF16)
        query_flat[PAIR * s : PAIR * (s + 1), :LAT] = latent
        query_flat[PAIR * s : PAIR * (s + 1), LAT:] = part[:, NOPE:]

    rows = H * RQ
    score_scale = (NOPE + ROPE) ** (-0.5)
    flat = query_flat[...]
    kept_all = kept[...].reshape(RQ * KB, row_width)
    row_scores = lax.dot_general(flat, kept_all, contract, preferred_element_type=F32)
    summ_scores = lax.dot_general(flat, summ[...], contract, preferred_element_type=F32)
    row_request = lax.broadcasted_iota(jnp.int32, (rows, RQ * KB), 0) & (RQ - 1)
    col_request = lax.broadcasted_iota(jnp.int32, (rows, RQ * KB), 1) // KB
    row_scores = jnp.where(row_request == col_request, row_scores * score_scale, NEGATIVE)
    summ_request = lax.broadcasted_iota(jnp.int32, (rows, PAIR), 0) & (RQ - 1)
    summ_column = lax.broadcasted_iota(jnp.int32, (rows, PAIR), 1)
    summ_scores = summ_scores * score_scale + jnp.log(F32(BLK - KB))
    summ_scores = jnp.where(summ_request == summ_column, summ_scores, NEGATIVE)
    maxima = jnp.maximum(
        jnp.max(row_scores, axis=1, keepdims=True), jnp.max(summ_scores, axis=1, keepdims=True)
    )
    row_weights = jnp.exp(row_scores - maxima)
    summ_weights = jnp.exp(summ_scores - maxima)
    totals = jnp.sum(row_weights, axis=1, keepdims=True) + jnp.sum(
        summ_weights, axis=1, keepdims=True
    )
    weighted = jnp.dot(
        row_weights.astype(BF16), kept_all[:, :LAT], preferred_element_type=F32
    ) + jnp.dot(summ_weights.astype(BF16), summ[:, :LAT], preferred_element_type=F32)
    live_rows = lax.broadcasted_iota(jnp.int32, (rows, 128), 0) & (RQ - 1)
    level = jnp.broadcast_to(maxima + jnp.log(totals), (rows, 128))
    for r in range(RQ):
        level = jnp.where((live_rows == r) & (owners[r] < 0), NEGATIVE, level)
    high = level.astype(BF16).astype(F32)
    middle = (level - high).astype(BF16).astype(F32)
    low = level - high - middle
    lane = lax.broadcasted_iota(jnp.int32, (rows, 128), 1)
    terms = jnp.where(
        lane == 0, high, jnp.where(lane == 1, middle, jnp.where(lane == 2, low, 0.0))
    )
    part_send[:, :, :LAT] = (weighted / totals).astype(BF16).reshape(seq_count, PAIR, LAT)
    part_send[:, :, LAT:] = terms.astype(BF16).reshape(seq_count, PAIR, 128)
    part_copies = [
        to_peer(
            part_send.at[seq_peer(k)],
            part_recv.at[me],
            p_send.at[k - 1],
            p_recv.at[k - 1],
            (seq_peer(k), my_mp),
        )
        for k in range(1, seq_count)
    ]
    part_recv[me] = part_send[me]

    total_rows = mp_count * RQ
    window_row = lax.broadcasted_iota(jnp.int32, (total_rows, 128), 0)
    window_low = jnp.zeros((total_rows, 128), jnp.int32)
    window_high = jnp.zeros((total_rows, 128), jnp.int32)
    for row in range(total_rows):
        tenant = ids_ref[row]
        window_low = jnp.where(window_row == row, ranges_ref[0, tenant], window_low)
        window_high = jnp.where(window_row == row, ranges_ref[1, tenant], window_high)
    vocab_start = (me * mp_count + my_mp) * vocab_width
    window_low = window_low - vocab_start
    window_high = window_high - vocab_start

    slot_source = [jnp.int32(0)] * slot_count
    for r in range(RQ):
        for b in range(block_count):
            offset = dest_ref[r, b] - me * slot_count
            for j in range(slot_count):
                slot_source[j] = jnp.where(offset == j, jnp.int32(b), slot_source[j])

    up_load.wait()
    for copy in part_copies:
        copy.wait_recv()
    pack_copies = [start_pack(k) for k in range(1, seq_count)]
    levels = [
        jnp.sum(part_recv[s, :, LAT:].astype(F32), axis=1, keepdims=True)
        for s in range(seq_count)
    ]
    peak = functools.reduce(jnp.maximum, levels)
    factors = [jnp.exp(part_level - peak) for part_level in levels]
    merged_sum = functools.reduce(
        jnp.add, [factors[s] * part_recv[s, :, :LAT].astype(F32) for s in range(seq_count)]
    )
    attended = (merged_sum / functools.reduce(jnp.add, factors)).astype(BF16).astype(F32)
    first_wide = lax.broadcasted_iota(jnp.int32, (PAIR, LAT), 0) < RQ
    split = jnp.concatenate(
        [jnp.where(first_wide, attended, 0.0), jnp.where(first_wide, 0.0, attended)], axis=1
    ).astype(BF16)
    values = jnp.dot(split, up_w[...].reshape(2 * LAT, VH), preferred_element_type=F32)
    value_recv[me] = values.astype(BF16)
    value_copies = [
        to_peer(
            value_recv.at[me],
            value_recv.at[me],
            v_send.at[k - 1],
            v_recv.at[k - 1],
            (seq_peer(k), my_mp),
        )
        for k in range(1, seq_count)
    ]
    out_load.wait()
    for copy in value_copies:
        copy.wait_recv()
    all_values = jnp.concatenate(
        [unfold(value_recv[s]) for s in range(seq_count)], axis=1
    ).astype(BF16)
    col_width = out_w.shape[1]
    residual = hidden_ref[:, pl.ds(pl.multiple_of(me * col_width, 128), col_width)]
    hidden = residual.astype(F32) + jnp.dot(all_values, out_w[...], preferred_element_type=F32)
    hidden = hidden.astype(BF16)
    hidden_out[...] = hidden
    hidden_all[my_mp, me] = fold(hidden.astype(F32)).astype(BF16)

    hidden_copies = [
        to_peer(
            hidden_all.at[my_mp, me],
            hidden_all.at[my_mp, me],
            h_send.at[k - 1],
            h_recv.at[k - 1],
            (seq_peer(k), my_mp),
        )
        for k in range(1, seq_count)
    ]
    for copy in hidden_copies:
        copy.wait_recv()
    group_copies = [
        to_peer(
            hidden_all.at[my_mp],
            hidden_all.at[my_mp],
            g_send.at[k - 1],
            g_recv.at[k - 1],
            (me, mp_peer(k)),
        )
        for k in range(1, mp_count)
    ]
    own_rows = jnp.concatenate(
        [unfold(hidden_all[my_mp, s]) for s in range(seq_count)], axis=1
    )
    own_norm = jnp.sqrt(jnp.mean(own_rows * own_rows, axis=1, keepdims=True))
    norm_out[...] = as_row(own_norm)
    gain = gain_ref[...].astype(F32).reshape(1, -1)
    for copy in group_copies:
        copy.wait_recv()
    normed = []
    for m in range(mp_count):
        group = jnp.concatenate([unfold(hidden_all[m, s]) for s in range(seq_count)], axis=1)
        mean_sq = jnp.mean(group * group, axis=1, keepdims=True)
        normed.append(group * lax.rsqrt(mean_sq + 1e-06) * gain)
    normed = jnp.concatenate(normed, axis=0).astype(BF16)

    head_load.wait()
    lane = lax.broadcasted_iota(jnp.int32, (total_rows, 128), 1)

    def head_step(n, best):
        start = pl.multiple_of(n * tile, 128)
        logits = jnp.dot(normed, head_w[:, pl.ds(start, tile)], preferred_element_type=F32)
        for i in range(tile // 128):
            column = lane + (start + i * 128)
            allowed = (column >= window_low) & (column < window_high)
            best = jnp.maximum(
                best, jnp.where(allowed, logits[:, i * 128 : (i + 1) * 128], NEGATIVE)
            )
        return best

    best = lax.fori_loop(
        0, vocab_width // tile, head_step, jnp.full((total_rows, 128), NEGATIVE, F32)
    )
    best = jnp.broadcast_to(jnp.max(best, axis=1, keepdims=True), (total_rows, 128))
    mp_best[...] = best.reshape(mp_count, RQ, 128)
    mp_best_recv[my_mp] = mp_best[my_mp]
    best_copies = [
        to_peer(
            mp_best.at[mp_peer(k)],
            mp_best_recv.at[my_mp],
            a_send.at[k - 1],
            a_recv.at[k - 1],
            (me, mp_peer(k)),
        )
        for k in range(1, mp_count)
    ]
    for copy in best_copies:
        copy.wait_recv()
    seq_best[me] = jnp.max(mp_best_recv[...], axis=0)
    last_copies = [
        to_peer(
            seq_best.at[me],
            seq_best.at[me],
            b_send.at[k - 1],
            b_recv.at[k - 1],
            (seq_peer(k), my_mp),
        )
        for k in range(1, seq_count)
    ]

    for copy in pack_copies:
        copy.wait_recv()
    lines = []
    for j in range(slot_count):
        source = slot_source[j]
        block = block_recv[source]
        for i in range(LAT // LANES):
            rows_out[j, :, i * LANES : (i + 1) * LANES] = block[i * KB : (i + 1) * KB]
        rope = block[ROPE_AT:SUMM_AT].astype(F32)
        rope = jnp.concatenate([rope[:, :ROPE], rope[:, ROPE:]], axis=0)
        rows_out[j, :, LAT:] = rope.astype(BF16)
        tail = block[SUMM_AT:].astype(F32)
        line = jnp.concatenate([tail[i : i + 1] for i in range(5)], axis=1)
        lines.append(line[:, :row_width])
    summary_out[...] = jnp.concatenate(lines, axis=0).astype(BF16)

    for copy in last_copies:
        copy.wait_recv()
    top_out[...] = as_row(jnp.max(seq_best[...], axis=0))
    for copy in (
        query_copies
        + pack_copies
        + part_copies
        + value_copies
        + hidden_copies
        + group_copies
        + best_copies
        + last_copies
    ):
        copy.wait_send()


def publish_kernel(*refs):
    results, places, sem = refs[:5], refs[5:10], refs[10]
    copies = [
        pltpu.make_async_copy(result, place, sem.at[i])
        for i, (result, place) in enumerate(zip(results, places))
    ]
    for copy in copies:
        copy.start()
    for copy in copies:
        copy.wait()


def fused_body(
    hidden_in,
    query_weight,
    key_absorb,
    value_up,
    out_weight,
    latent_cache,
    cache_lengths,
    keep_lists,
    drop_weights,
    pack_dest,
    final_gain,
    head_weight,
    tenant_ranges,
    tenant_ids,
):
    seq_count = lax.axis_size("seq")
    mp_count = lax.axis_size("mp")
    row_width = LAT + ROPE
    slot_count = RQ // 2
    depth, vocab_width = head_weight.shape
    tile = next(t for t in (640, 512, 384, 256, 128) if vocab_width % t == 0)
    vmem = pl.BlockSpec(memory_space=pltpu.VMEM)
    smem = pl.BlockSpec(memory_space=pltpu.SMEM)
    hbm = pl.BlockSpec(memory_space=pltpu.HBM)
    seq_sems = pltpu.SemaphoreType.DMA((seq_count - 1,))
    mp_sems = pltpu.SemaphoreType.DMA((mp_count - 1,))
    outs = pl.pallas_call(
        functools.partial(layer_kernel, seq_count, mp_count, vocab_width, tile),
        out_shape=(
            jax.ShapeDtypeStruct((slot_count, KB, row_width), BF16),
            jax.ShapeDtypeStruct((slot_count, row_width), BF16),
            jax.ShapeDtypeStruct((RQ, out_weight.shape[1]), BF16),
            jax.ShapeDtypeStruct((1, RQ), F32),
            jax.ShapeDtypeStruct((1, RQ), F32),
        ),
        in_specs=[vmem] * 4 + [smem] * 3 + [hbm] * 6,
        out_specs=(vmem,) * 5,
        scratch_shapes=[
            pltpu.VMEM(query_weight.shape, BF16),
            pltpu.VMEM(key_absorb.shape, BF16),
            pltpu.VMEM((2,) + value_up.shape[1:], BF16),
            pltpu.VMEM(out_weight.shape, BF16),
            pltpu.VMEM((RQ, row_width, BLK), BF16),
            pltpu.VMEM(head_weight.shape, BF16),
            pltpu.VMEM((seq_count, PAIR, NOPE + ROPE), BF16),
            pltpu.VMEM((H * RQ, row_width), BF16),
            pltpu.VMEM((RQ, KB, row_width), BF16),
            pltpu.VMEM((PAIR, row_width), BF16),
            pltpu.VMEM((RQ, MESSAGE, LANES), BF16),
            pltpu.VMEM((seq_count - 1, MESSAGE, LANES), BF16),
            pltpu.VMEM((seq_count, MESSAGE, LANES), BF16),
            pltpu.VMEM((seq_count, PAIR, LAT + 128), BF16),
            pltpu.VMEM((seq_count, PAIR, LAT + 128), BF16),
            pltpu.VMEM((seq_count, PAIR, VH), BF16),
            pltpu.VMEM((mp_count, seq_count, PAIR, out_weight.shape[1] // 2), BF16),
            pltpu.VMEM((mp_count, RQ, 128), F32),
            pltpu.VMEM((mp_count, RQ, 128), F32),
            pltpu.VMEM((seq_count, RQ, 128), F32),
            pltpu.SemaphoreType.DMA((6,)),
        ]
        + [seq_sems] * 10
        + [mp_sems] * 4
        + [seq_sems] * 2,
        compiler_params=pltpu.CompilerParams(
            collective_id=0, has_side_effects=True, vmem_limit_bytes=213 * 2**18
        ),
    )(
        hidden_in,
        keep_lists,
        drop_weights,
        final_gain,
        pack_dest,
        jnp.swapaxes(tenant_ranges, 0, 1),
        tenant_ids,
        query_weight,
        key_absorb,
        value_up,
        out_weight,
        jnp.swapaxes(latent_cache, 1, 2),
        head_weight,
    )
    outs = pl.pallas_call(
        publish_kernel,
        out_shape=tuple(jax.ShapeDtypeStruct(out.shape, out.dtype) for out in outs),
        in_specs=[vmem] * 5,
        out_specs=(hbm,) * 5,
        scratch_shapes=[pltpu.SemaphoreType.DMA((5,))],
    )(*outs)
    packed_rows, packed_summary, hidden_out, state_norm, top_logit = outs
    return (
        packed_rows,
        packed_summary,
        hidden_out,
        state_norm.reshape(RQ),
        top_logit.reshape(RQ),
    )


def solution(mesh):
    in_specs = (
        P("mp", None),
        P(None, "seq"),
        P(),
        P(),
        P(None, "seq"),
        P("mp", "seq", None),
        P("mp"),
        P("mp", "seq", None),
        P("mp", "seq"),
        P("mp", None),
        P(),
        P(None, ("seq", "mp")),
        P(),
        P(),
    )
    out_specs = (
        P(("seq", "mp"), None, None),
        P(("seq", "mp"), None),
        P("mp", "seq"),
        P("mp"),
        P("mp"),
    )
    seq_count = mesh.shape["seq"]
    fused = seq_count * 2 == H
    return jax.shard_map(fused_body if fused else body, mesh=mesh, in_specs=in_specs, out_specs=out_specs, check_vma=False)
```

```python
import functools

import jax
import jax.numpy as jnp
from jax import lax
from jax.experimental import pallas as pl
from jax.experimental.pallas import tpu as pltpu
from jax.sharding import PartitionSpec as P

H = 16
NOPE = 128
ROPE = 64
LAT = 512
VH = 128
BLK = 128
KB = 64
TENANTS = 4
RQ = 8


NEGATIVE = -1e30
HIGHEST = lax.Precision.HIGHEST


def merged(x, axis, combine):
    everything = jax.tree.map(lambda part: lax.all_gather(part, axis), x)
    initial = jax.tree.map(lambda part: part[0], everything)

    def step(k, so_far):
        return combine(so_far, jax.tree.map(lambda part: part[k], everything))

    return lax.fori_loop(1, lax.axis_size(axis), step, initial)


def compact_blocks(block_rows, keep_onehot, weights_dropped):
    kept_rows = jnp.einsum(
        "nkt,ntc->nkc", keep_onehot, block_rows, preferred_element_type=jnp.float32
    ).astype(jnp.bfloat16)
    weight_mass = jnp.sum(weights_dropped.astype(jnp.float32), axis=1)
    summed = jnp.einsum(
        "nt,ntc->nc", weights_dropped, block_rows, preferred_element_type=jnp.float32
    )
    summary = (summed / weight_mass[:, None]).astype(jnp.bfloat16)
    return (kept_rows, summary)


def attend_blocks(query_lat, query_rope, kept_rows, summary, usable):
    score_scale = (NOPE + ROPE) ** (-0.5)
    row_scores = (
        jnp.einsum(
            "nhl,nkl->nhk", query_lat, kept_rows[:, :, :LAT], preferred_element_type=jnp.float32
        )
        + jnp.einsum(
            "nhr,nkr->nhk", query_rope, kept_rows[:, :, LAT:], preferred_element_type=jnp.float32
        )
    ) * score_scale
    summ_scores = (
        jnp.einsum("nhl,nl->nh", query_lat, summary[:, :LAT], preferred_element_type=jnp.float32)
        + jnp.einsum("nhr,nr->nh", query_rope, summary[:, LAT:], preferred_element_type=jnp.float32)
    ) * score_scale
    summ_scores = summ_scores + jnp.log(jnp.float32(BLK - KB))
    row_scores = jnp.where(usable[:, None, None], row_scores, NEGATIVE)
    summ_scores = jnp.where(usable[:, None], summ_scores, NEGATIVE)
    maxima = jnp.maximum(jnp.max(row_scores, axis=2), summ_scores)
    row_weights = jnp.where(usable[:, None, None], jnp.exp(row_scores - maxima[:, :, None]), 0.0)
    summ_weights = jnp.where(usable[:, None], jnp.exp(summ_scores - maxima), 0.0)
    totals = jnp.sum(row_weights, axis=2) + summ_weights
    weighted = jnp.einsum(
        "nhk,nkl->nhl", row_weights, kept_rows[:, :, :LAT].astype(jnp.float32), precision=HIGHEST
    )
    weighted = weighted + summ_weights[:, :, None] * summary[:, None, :LAT].astype(jnp.float32)
    return (maxima, totals, weighted)


def per_request(maxima, totals, weighted, owner_of):
    request_max = jnp.max(jnp.where(owner_of[:, :, None], maxima[None, :, :], NEGATIVE), axis=1)
    shifted = jnp.where(owner_of[:, :, None], maxima[None, :, :] - request_max[:, None, :], 0.0)
    factor = jnp.where(owner_of[:, :, None], jnp.exp(shifted), 0.0)
    request_total = jnp.einsum("rnh,nh->rh", factor, totals, precision=HIGHEST)
    request_sum = jnp.einsum("rnh,nhl->rhl", factor, weighted, precision=HIGHEST)
    return (request_max, request_total, request_sum)


def combine_partial(former, latter):
    former_max, former_total, former_sum = former
    latter_max, latter_total, latter_sum = latter
    joined = jnp.maximum(former_max, latter_max)
    former_factor = jnp.exp(former_max - joined)
    latter_factor = jnp.exp(latter_max - joined)
    return (
        joined,
        former_factor * former_total + latter_factor * latter_total,
        former_factor[:, :, None] * former_sum + latter_factor[:, :, None] * latter_sum,
    )


def body(
    hidden_in,
    query_weight,
    key_absorb,
    value_up,
    out_weight,
    latent_cache,
    cache_lengths,
    keep_lists,
    drop_weights,
    pack_dest,
    final_gain,
    head_weight,
    tenant_ranges,
    tenant_ids,
):
    seq_count = lax.axis_size("seq")
    mp_count = lax.axis_size("mp")
    seq_index = lax.axis_index("seq")
    mp_index = lax.axis_index("mp")
    capacity = max(1, RQ // seq_count)
    slot_count = RQ // 2
    row_width = LAT + ROPE
    query_part = jnp.dot(hidden_in, query_weight, preferred_element_type=jnp.float32).astype(
        jnp.bfloat16
    )
    query_full = lax.all_gather(query_part, "seq", axis=1, tiled=True).reshape(RQ, H, NOPE + ROPE)
    query_lat = jnp.einsum(
        "rhn,hnl->rhl", query_full[:, :, :NOPE], key_absorb, preferred_element_type=jnp.float32
    ).astype(jnp.bfloat16)
    query_rope = query_full[:, :, NOPE:]
    positions = jnp.arange(BLK, dtype=jnp.int32)
    keep_onehot = keep_lists[:, 0, :, None] == positions[None, None, :]
    kept_flag = jnp.sum(keep_onehot.astype(jnp.int32), axis=1)
    weights_dropped = (drop_weights * (1 - kept_flag)).astype(jnp.bfloat16)
    live_here = cache_lengths > seq_index * BLK
    dest_here = lax.dynamic_slice_in_dim(pack_dest, seq_index, 1, 1)[:, 0]
    send_slot = dest_here // slot_count * capacity + dest_here % slot_count % capacity
    slot_range = jnp.arange(seq_count * capacity, dtype=jnp.int32)
    send_onehot = ((send_slot[None, :] == slot_range[:, None]) & live_here[None, :]).astype(
        jnp.bfloat16
    )
    targets = seq_index * slot_count + jnp.arange(slot_count, dtype=jnp.int32)
    slot_match = (pack_dest[None, :, :] == targets[:, None, None]).astype(jnp.int32)
    block_range = jnp.arange(pack_dest.shape[1], dtype=jnp.int32)
    source_of = jnp.sum(slot_match * block_range[None, None, :], axis=(1, 2))
    request_of = jnp.sum(slot_match, axis=2)
    request_index = jnp.sum(request_of * jnp.arange(RQ, dtype=jnp.int32)[None, :], axis=1)
    pick_index = source_of * capacity + jnp.arange(slot_count, dtype=jnp.int32) % capacity
    owner_of = jnp.transpose(request_of) > 0
    local_rows, local_summary = compact_blocks(
        latent_cache, keep_onehot.astype(jnp.bfloat16), weights_dropped
    )
    send_rows = jnp.einsum(
        "jr,rkc->jkc", send_onehot, local_rows, preferred_element_type=jnp.float32
    )
    send_rows = send_rows.astype(jnp.bfloat16).reshape(seq_count, capacity, KB, row_width)
    send_summary = jnp.dot(send_onehot, local_summary, preferred_element_type=jnp.float32)
    send_summary = send_summary.astype(jnp.bfloat16).reshape(seq_count, capacity, row_width)
    recv_rows, recv_summary = (
        lax.all_to_all(send_rows, "seq", split_axis=0, concat_axis=0, tiled=True),
        lax.all_to_all(send_summary, "seq", split_axis=0, concat_axis=0, tiled=True),
    )
    packed_rows = jnp.take(
        recv_rows.reshape(seq_count * capacity, KB, row_width), pick_index, axis=0
    )
    packed_summary = jnp.take(
        recv_summary.reshape(seq_count * capacity, row_width), pick_index, axis=0
    )
    slot_query_lat = jnp.take(query_lat, request_index, axis=0)
    slot_query_rope = jnp.take(query_rope, request_index, axis=0)
    usable = jnp.ones((slot_count,), dtype=bool)
    maxima, totals, weighted = attend_blocks(
        slot_query_lat, slot_query_rope, packed_rows, packed_summary, usable
    )
    partial_value = per_request(maxima, totals, weighted, owner_of)
    request_max, request_total, request_sum = merged(partial_value, "seq", combine_partial)
    attended = (request_sum / request_total[:, :, None]).astype(jnp.bfloat16)
    values = jnp.einsum("rhl,hlv->rhv", attended, value_up, preferred_element_type=jnp.float32)
    values = values.astype(jnp.bfloat16).reshape(RQ, H * VH)
    col_width = out_weight.shape[1]
    residual = lax.dynamic_slice_in_dim(hidden_in, seq_index * col_width, col_width, 1)
    hidden_out = (
        residual.astype(jnp.float32)
        + jnp.dot(values, out_weight, preferred_element_type=jnp.float32)
    ).astype(jnp.bfloat16)
    gathered = lax.all_gather(hidden_out[None], ("seq", "mp"), axis=0, tiled=True)
    all_rows = gathered.reshape(seq_count, mp_count, RQ, col_width).transpose(1, 2, 0, 3)
    all_rows = all_rows.reshape(mp_count * RQ, seq_count * col_width)
    rows_f = all_rows.astype(jnp.float32)
    mean_sq = jnp.mean(rows_f * rows_f, axis=1)
    norms_all = jnp.sqrt(mean_sq)
    normed = (
        rows_f * lax.rsqrt(mean_sq + 1e-06)[:, None] * final_gain.astype(jnp.float32)[None, :]
    ).astype(jnp.bfloat16)
    logits = jnp.dot(normed, head_weight, preferred_element_type=jnp.float32)
    vocab_width = head_weight.shape[1]
    device_index = seq_index * mp_count + mp_index
    columns = device_index * vocab_width + jnp.arange(vocab_width, dtype=jnp.int32)
    tenant_onehot = (tenant_ids[:, None] == jnp.arange(TENANTS, dtype=jnp.int32)[None, :]).astype(
        jnp.int32
    )
    window_low = jnp.sum(tenant_onehot * tenant_ranges[None, :, 0], axis=1)
    window_high = jnp.sum(tenant_onehot * tenant_ranges[None, :, 1], axis=1)
    allowed = (columns[None, :] >= window_low[:, None]) & (columns[None, :] < window_high[:, None])
    local_best = jnp.max(jnp.where(allowed, logits, NEGATIVE), axis=1)
    best_all = lax.pmax(local_best, ("seq", "mp"))
    row_start = mp_index * RQ
    state_norm = lax.dynamic_slice_in_dim(norms_all, row_start, RQ, 0)
    top_logit = lax.dynamic_slice_in_dim(best_all, row_start, RQ, 0)
    return (packed_rows, packed_summary, hidden_out, state_norm, top_logit)


F32 = jnp.float32
BF16 = jnp.bfloat16
PAIR = 2 * RQ
LANES = 128
ROPE_AT = LAT // LANES * KB
SUMM_AT = ROPE_AT + KB // 2
MESSAGE = SUMM_AT + PAIR


def to_peer(src, dst, send_sem, recv_sem, device):
    copy = pltpu.make_async_remote_copy(
        src_ref=src,
        dst_ref=dst,
        send_sem=send_sem,
        recv_sem=recv_sem,
        device_id=device,
        device_id_type=pl.DeviceIdType.MESH,
    )
    copy.start()
    return copy


def as_row(column):
    wide = jnp.broadcast_to(column[:, :1], (RQ, RQ))
    sub = lax.broadcasted_iota(jnp.int32, (RQ, RQ), 0)
    lane = lax.broadcasted_iota(jnp.int32, (RQ, RQ), 1)
    return jnp.sum(jnp.where(sub == lane, wide, 0.0), axis=0, keepdims=True)


def unfold(part):
    wide = part.astype(F32)
    return jnp.concatenate([wide[:RQ], wide[RQ:]], axis=1)


def fold(x):
    width = x.shape[1] // 2
    return jnp.concatenate([x[:, :width], x[:, width:]], axis=0)


def layer_kernel(
    seq_count,
    mp_count,
    vocab_width,
    tile,
    hidden_hbm,
    keep_hbm,
    drop_hbm,
    gain_hbm,
    dest_hbm,
    ranges_hbm,
    ids_hbm,
    query_hbm,
    absorb_hbm,
    up_hbm,
    out_hbm,
    cache_hbm,
    head_hbm,
    rows_hbm,
    summary_hbm,
    hidden_out_hbm,
    norm_hbm,
    top_hbm,
    hidden_ref,
    keep_ref,
    drop_ref,
    gain_ref,
    dest_ref,
    ranges_ref,
    ids_ref,
    rows_out,
    summary_out,
    hidden_out,
    norm_out,
    top_out,
    query_w,
    absorb_w,
    up_w,
    out_w,
    cache,
    head_w,
    query_recv,
    query_flat,
    kept,
    summ,
    blocks,
    block_send,
    block_recv,
    part_send,
    part_recv,
    value_recv,
    hidden_all,
    best_all,
    local_sem,
    store_sem,
    q_send,
    q_recv,
    r_send,
    r_recv,
    p_send,
    p_recv,
    v_send,
    v_recv,
    h_send,
    h_recv,
    g_send,
    g_recv,
    b_send,
    b_recv,
):
    me = lax.axis_index("seq")
    my_mp = lax.axis_index("mp")
    slot_count = RQ // 2
    block_count = dest_ref.shape[1]
    row_width = LAT + ROPE
    contract = (((1,), (1,)), ((), ()))

    def seq_peer(k):
        return lax.rem(me + k, seq_count)

    def mp_peer(k):
        return lax.rem(my_mp + k, mp_count)

    def load(i, src, dst):
        copy = pltpu.make_async_copy(src, dst, local_sem.at[i])
        copy.start()
        return copy

    keep_load = load(0, keep_hbm, keep_ref)
    drop_load = load(1, drop_hbm, drop_ref)
    hidden_load = load(2, hidden_hbm, hidden_ref)
    query_load = load(3, query_hbm, query_w)
    dest_load = load(4, dest_hbm, dest_ref)
    cache_load = load(5, cache_hbm, cache)
    gain_load = load(6, gain_hbm, gain_ref)
    ranges_load = load(7, ranges_hbm, ranges_ref)
    ids_load = load(8, ids_hbm, ids_ref)
    absorb_load = load(9, absorb_hbm, absorb_w)

    def other(k):
        place = lax.rem(me * mp_count + my_mp + k, seq_count * mp_count)
        return (place // mp_count, lax.rem(place, mp_count))

    device_count = seq_count * mp_count
    barrier = pltpu.get_barrier_semaphore()
    for k in range(1, device_count):
        pl.semaphore_signal(
            barrier, inc=1, device_id=other(k), device_id_type=pl.DeviceIdType.MESH
        )
    keep_load.wait()
    drop_load.wait()

    keep = jnp.concatenate([keep_ref[:, 0, :], keep_ref[:, 0, :]], axis=1).astype(F32)
    keep_t = jnp.transpose(keep)[:KB]
    position = lax.broadcasted_iota(jnp.int32, (KB, BLK), 1).astype(F32)
    request_sub = lax.broadcasted_iota(jnp.int32, (RQ, BLK), 0)
    picks = []
    kept_flag = jnp.zeros((RQ, BLK), F32)
    for r in range(RQ):
        pick = jnp.where(jnp.broadcast_to(keep_t[:, r : r + 1], (KB, BLK)) == position, 1.0, 0.0)
        flag = jnp.sum(pick, axis=0, keepdims=True)
        kept_flag = jnp.where(request_sub == r, jnp.broadcast_to(flag, (RQ, BLK)), kept_flag)
        picks.append(pick)
    dropped = drop_ref[...].astype(F32) * (1.0 - kept_flag)
    mass = jnp.sum(dropped, axis=1, keepdims=True)

    hidden_load.wait()
    query_load.wait()
    query = jnp.dot(hidden_ref[...], query_w[...], preferred_element_type=F32)
    query_recv[me] = fold(query).astype(BF16)
    pl.semaphore_wait(barrier, device_count - 1)
    query_copies = [
        to_peer(
            query_recv.at[me],
            query_recv.at[me],
            q_send.at[k - 1],
            q_recv.at[k - 1],
            (seq_peer(k), my_mp),
        )
        for k in range(1, seq_count)
    ]
    out_load = load(10, out_hbm, out_w)
    up_load = load(11, up_hbm.at[pl.ds(me * 2, 2)], up_w)
    head_load = load(12, head_hbm, head_w)

    cache_load.wait()
    summed = jnp.zeros((PAIR, row_width), F32)
    pad = jnp.zeros((PAIR - RQ, BLK), F32)
    for r in range(RQ):
        own = jnp.where(request_sub == r, dropped, 0.0)
        both = jnp.concatenate([picks[r], own, pad], axis=0).astype(BF16)
        chosen = lax.dot_general(both, cache[r], contract, preferred_element_type=F32)
        summed = summed + chosen[KB:]
        chosen = chosen[:KB]
        kept[r] = chosen.astype(BF16)
        for i in range(LAT // LANES):
            piece = chosen[:, i * LANES : (i + 1) * LANES]
            blocks[r, i * KB : (i + 1) * KB, :] = piece.astype(BF16)
        rope = chosen[:, LAT:]
        rope = jnp.concatenate([rope[: KB // 2], rope[KB // 2 :]], axis=1)
        blocks[r, ROPE_AT:SUMM_AT, :] = rope.astype(BF16)
    mass_pair = jnp.concatenate([mass, jnp.ones_like(mass)], axis=0)
    summary = (summed / mass_pair).astype(BF16)
    summ[...] = summary
    summary_f = summary.astype(F32)[:RQ]
    summary_f = jnp.concatenate(
        [summary_f, jnp.zeros((RQ, 5 * LANES - row_width), F32)], axis=1
    )
    line = lax.broadcasted_iota(jnp.int32, (PAIR, LANES), 0)
    for r in range(RQ):
        lines = jnp.zeros((PAIR, LANES), F32)
        for i in range(5):
            piece = summary_f[r : r + 1, i * LANES : (i + 1) * LANES]
            lines = jnp.where(line == i, jnp.broadcast_to(piece, (PAIR, LANES)), lines)
        blocks[r, SUMM_AT:, :] = lines.astype(BF16)

    dest_load.wait()
    owners = [dest_ref[r, me] >> 2 for r in range(RQ)]

    def request_for(owner):
        chosen = jnp.int32(0)
        for r in range(RQ):
            chosen = jnp.where(owners[r] == owner, jnp.int32(r), chosen)
        return chosen

    block_recv[me] = blocks[request_for(me)]
    for k in range(1, seq_count):
        block_send[k - 1] = blocks[request_for(seq_peer(k))]

    def start_pack(k):
        return to_peer(
            block_send.at[k - 1],
            block_recv.at[me],
            r_send.at[k - 1],
            r_recv.at[k - 1],
            (seq_peer(k), my_mp),
        )

    absorb_load.wait()
    for copy in query_copies:
        copy.wait_recv()
    early = (1, seq_count - 1)
    pack_copies = [start_pack(k) for k in early]
    first_half = lax.broadcasted_iota(jnp.int32, (PAIR, NOPE), 0) < RQ
    for s in range(seq_count):
        part = query_recv[s]
        nope = part[:, :NOPE].astype(F32)
        split = jnp.concatenate(
            [jnp.where(first_half, nope, 0.0), jnp.where(first_half, 0.0, nope)], axis=1
        ).astype(BF16)
        weight = absorb_w[2 * s : 2 * s + 2].reshape(2 * NOPE, LAT)
        latent = jnp.dot(split, weight, preferred_element_type=F32).astype(BF16)
        query_flat[PAIR * s : PAIR * (s + 1), :LAT] = latent
        query_flat[PAIR * s : PAIR * (s + 1), LAT:] = part[:, NOPE:]

    rows = H * RQ
    score_scale = (NOPE + ROPE) ** (-0.5)
    flat = query_flat[...]
    kept_all = kept[...].reshape(RQ * KB, row_width)
    row_scores = lax.dot_general(flat, kept_all, contract, preferred_element_type=F32)
    summ_scores = lax.dot_general(flat, summ[...], contract, preferred_element_type=F32)
    row_request = lax.broadcasted_iota(jnp.int32, (rows, RQ * KB), 0) & (RQ - 1)
    col_request = lax.broadcasted_iota(jnp.int32, (rows, RQ * KB), 1) // KB
    row_scores = jnp.where(row_request == col_request, row_scores * score_scale, NEGATIVE)
    summ_request = lax.broadcasted_iota(jnp.int32, (rows, PAIR), 0) & (RQ - 1)
    summ_column = lax.broadcasted_iota(jnp.int32, (rows, PAIR), 1)
    summ_scores = summ_scores * score_scale + jnp.log(F32(BLK - KB))
    summ_scores = jnp.where(summ_request == summ_column, summ_scores, NEGATIVE)
    maxima = jnp.maximum(
        jnp.max(row_scores, axis=1, keepdims=True), jnp.max(summ_scores, axis=1, keepdims=True)
    )
    row_weights = jnp.exp(row_scores - maxima)
    summ_weights = jnp.exp(summ_scores - maxima)
    totals = jnp.sum(row_weights, axis=1, keepdims=True) + jnp.sum(
        summ_weights, axis=1, keepdims=True
    )
    weighted = jnp.dot(
        row_weights.astype(BF16), kept_all[:, :LAT], preferred_element_type=F32
    ) + jnp.dot(summ_weights.astype(BF16), summ[:, :LAT], preferred_element_type=F32)
    live_rows = lax.broadcasted_iota(jnp.int32, (rows, 128), 0) & (RQ - 1)
    level = jnp.broadcast_to(maxima + jnp.log(totals), (rows, 128))
    for r in range(RQ):
        level = jnp.where((live_rows == r) & (owners[r] < 0), NEGATIVE, level)
    high = level.astype(BF16).astype(F32)
    middle = (level - high).astype(BF16).astype(F32)
    low = level - high - middle
    lane = lax.broadcasted_iota(jnp.int32, (rows, 128), 1)
    terms = jnp.where(
        lane == 0, high, jnp.where(lane == 1, middle, jnp.where(lane == 2, low, 0.0))
    )
    part_send[:, :, :LAT] = (weighted / totals).astype(BF16).reshape(seq_count, PAIR, LAT)
    part_send[:, :, LAT:] = terms.astype(BF16).reshape(seq_count, PAIR, 128)
    part_copies = [
        to_peer(
            part_send.at[seq_peer(k)],
            part_recv.at[me],
            p_send.at[k - 1],
            p_recv.at[k - 1],
            (seq_peer(k), my_mp),
        )
        for k in range(1, seq_count)
    ]
    part_recv[me] = part_send[me]

    ranges_load.wait()
    ids_load.wait()
    total_rows = mp_count * RQ
    window_row = lax.broadcasted_iota(jnp.int32, (total_rows, 128), 0)
    window_low = jnp.zeros((total_rows, 128), jnp.int32)
    window_high = jnp.zeros((total_rows, 128), jnp.int32)
    for row in range(total_rows):
        tenant = ids_ref[row]
        window_low = jnp.where(window_row == row, ranges_ref[0, tenant], window_low)
        window_high = jnp.where(window_row == row, ranges_ref[1, tenant], window_high)
    vocab_start = (me * mp_count + my_mp) * vocab_width
    window_low = window_low - vocab_start
    window_high = window_high - vocab_start

    slot_source = [jnp.int32(0)] * slot_count
    for r in range(RQ):
        for b in range(block_count):
            offset = dest_ref[r, b] - me * slot_count
            for j in range(slot_count):
                slot_source[j] = jnp.where(offset == j, jnp.int32(b), slot_source[j])

    up_load.wait()
    for copy in part_copies:
        copy.wait_recv()
    pack_copies += [start_pack(k) for k in range(1, seq_count) if k not in early]
    levels = [
        jnp.sum(part_recv[s, :, LAT:].astype(F32), axis=1, keepdims=True)
        for s in range(seq_count)
    ]
    peak = functools.reduce(jnp.maximum, levels)
    factors = [jnp.exp(part_level - peak) for part_level in levels]
    merged_sum = functools.reduce(
        jnp.add, [factors[s] * part_recv[s, :, :LAT].astype(F32) for s in range(seq_count)]
    )
    attended = (merged_sum / functools.reduce(jnp.add, factors)).astype(BF16).astype(F32)
    first_wide = lax.broadcasted_iota(jnp.int32, (PAIR, LAT), 0) < RQ
    split = jnp.concatenate(
        [jnp.where(first_wide, attended, 0.0), jnp.where(first_wide, 0.0, attended)], axis=1
    ).astype(BF16)
    values = jnp.dot(split, up_w[...].reshape(2 * LAT, VH), preferred_element_type=F32)
    value_recv[me] = values.astype(BF16)
    value_copies = [
        to_peer(
            value_recv.at[me],
            value_recv.at[me],
            v_send.at[k - 1],
            v_recv.at[k - 1],
            (seq_peer(k), my_mp),
        )
        for k in range(1, seq_count)
    ]
    out_load.wait()
    for copy in value_copies:
        copy.wait_recv()
    all_values = jnp.concatenate(
        [unfold(value_recv[s]) for s in range(seq_count)], axis=1
    ).astype(BF16)
    col_width = out_w.shape[1]
    residual = hidden_ref[:, pl.ds(pl.multiple_of(me * col_width, 128), col_width)]
    hidden = residual.astype(F32) + jnp.dot(all_values, out_w[...], preferred_element_type=F32)
    hidden = hidden.astype(BF16)
    hidden_out[...] = hidden

    def store(i, src, dst):
        copy = pltpu.make_async_copy(src, dst, store_sem.at[i])
        copy.start()
        return copy

    stores = [store(0, hidden_out, hidden_out_hbm)]
    hidden_all[my_mp, me] = fold(hidden.astype(F32)).astype(BF16)

    hidden_copies = [
        to_peer(
            hidden_all.at[my_mp, me],
            hidden_all.at[my_mp, me],
            h_send.at[k - 1],
            h_recv.at[k - 1],
            (seq_peer(k), my_mp),
        )
        for k in range(1, seq_count)
    ]
    for copy in hidden_copies:
        copy.wait_recv()
    group_copies = [
        to_peer(
            hidden_all.at[my_mp],
            hidden_all.at[my_mp],
            g_send.at[k - 1],
            g_recv.at[k - 1],
            (me, mp_peer(k)),
        )
        for k in range(1, mp_count)
    ]
    own_rows = jnp.concatenate(
        [unfold(hidden_all[my_mp, s]) for s in range(seq_count)], axis=1
    )
    own_norm = jnp.sqrt(jnp.mean(own_rows * own_rows, axis=1, keepdims=True))
    norm_out[...] = as_row(own_norm)
    stores.append(store(1, norm_out, norm_hbm))
    gain_load.wait()
    gain = gain_ref[...].astype(F32).reshape(1, -1)
    for copy in group_copies:
        copy.wait_recv()
    normed = []
    for m in range(mp_count):
        group = jnp.concatenate([unfold(hidden_all[m, s]) for s in range(seq_count)], axis=1)
        mean_sq = jnp.mean(group * group, axis=1, keepdims=True)
        normed.append(group * lax.rsqrt(mean_sq + 1e-06) * gain)
    normed = jnp.concatenate(normed, axis=0).astype(BF16)

    head_load.wait()
    lane = lax.broadcasted_iota(jnp.int32, (total_rows, 128), 1)

    def head_step(n, best):
        start = pl.multiple_of(n * tile, 128)
        logits = jnp.dot(normed, head_w[:, pl.ds(start, tile)], preferred_element_type=F32)
        for i in range(tile // 128):
            column = lane + (start + i * 128)
            allowed = (column >= window_low) & (column < window_high)
            best = jnp.maximum(
                best, jnp.where(allowed, logits[:, i * 128 : (i + 1) * 128], NEGATIVE)
            )
        return best

    best = lax.fori_loop(
        0, vocab_width // tile, head_step, jnp.full((total_rows, 128), NEGATIVE, F32)
    )
    best = jnp.broadcast_to(jnp.max(best, axis=1, keepdims=True), (total_rows, 128))
    diagonal = window_row == lane
    here = me * mp_count + my_mp
    best_all[here] = jnp.sum(jnp.where(diagonal, best, 0.0), axis=0, keepdims=True)
    best_copies = [
        to_peer(
            best_all.at[here], best_all.at[here], b_send.at[k - 1], b_recv.at[k - 1], other(k)
        )
        for k in range(1, device_count)
    ]

    for copy in pack_copies:
        copy.wait_recv()
    lines = []
    for j in range(slot_count):
        source = slot_source[j]
        block = block_recv[source]
        for i in range(LAT // LANES):
            rows_out[j, :, i * LANES : (i + 1) * LANES] = block[i * KB : (i + 1) * KB]
        rope = block[ROPE_AT:SUMM_AT].astype(F32)
        rope = jnp.concatenate([rope[:, :ROPE], rope[:, ROPE:]], axis=0)
        rows_out[j, :, LAT:] = rope.astype(BF16)
        tail = block[SUMM_AT:].astype(F32)
        line = jnp.concatenate([tail[i : i + 1] for i in range(5)], axis=1)
        lines.append(line[:, :row_width])
    summary_out[...] = jnp.concatenate(lines, axis=0).astype(BF16)
    stores.append(store(2, rows_out, rows_hbm))
    stores.append(store(3, summary_out, summary_hbm))

    for copy in best_copies:
        copy.wait_recv()
    top = jnp.max(best_all[...], axis=0)
    own_top = top[:, :RQ]
    for m in range(1, mp_count):
        own_top = jnp.where(my_mp == m, top[:, m * RQ : (m + 1) * RQ], own_top)
    top_out[...] = own_top
    stores.append(store(4, top_out, top_hbm))
    for copy in (
        query_copies
        + pack_copies
        + part_copies
        + value_copies
        + hidden_copies
        + group_copies
        + best_copies
    ):
        copy.wait_send()
    for copy in stores:
        copy.wait()


def publish_kernel(*refs):
    results, places, sem = refs[:5], refs[5:10], refs[10]
    copies = [
        pltpu.make_async_copy(result, place, sem.at[i])
        for i, (result, place) in enumerate(zip(results, places))
    ]
    for copy in copies:
        copy.start()
    for copy in copies:
        copy.wait()


def fused_body(
    hidden_in,
    query_weight,
    key_absorb,
    value_up,
    out_weight,
    latent_cache,
    cache_lengths,
    keep_lists,
    drop_weights,
    pack_dest,
    final_gain,
    head_weight,
    tenant_ranges,
    tenant_ids,
):
    seq_count = lax.axis_size("seq")
    mp_count = lax.axis_size("mp")
    row_width = LAT + ROPE
    slot_count = RQ // 2
    depth, vocab_width = head_weight.shape
    tile = next(t for t in (640, 512, 384, 256, 128) if vocab_width % t == 0)
    hbm = pl.BlockSpec(memory_space=pltpu.HBM)
    seq_sems = pltpu.SemaphoreType.DMA((seq_count - 1,))
    all_sems = pltpu.SemaphoreType.DMA((seq_count * mp_count - 1,))
    mp_sems = pltpu.SemaphoreType.DMA((mp_count - 1,))
    outs = pl.pallas_call(
        functools.partial(layer_kernel, seq_count, mp_count, vocab_width, tile),
        out_shape=(
            jax.ShapeDtypeStruct((slot_count, KB, row_width), BF16),
            jax.ShapeDtypeStruct((slot_count, row_width), BF16),
            jax.ShapeDtypeStruct((RQ, out_weight.shape[1]), BF16),
            jax.ShapeDtypeStruct((1, RQ), F32),
            jax.ShapeDtypeStruct((1, RQ), F32),
        ),
        in_specs=[hbm] * 13,
        out_specs=(hbm,) * 5,
        scratch_shapes=[
            pltpu.VMEM(hidden_in.shape, BF16),
            pltpu.VMEM(keep_lists.shape, jnp.int32),
            pltpu.VMEM(drop_weights.shape, jnp.int32),
            pltpu.VMEM(final_gain.shape, BF16),
            pltpu.SMEM(pack_dest.shape, jnp.int32),
            pltpu.SMEM((2, TENANTS), jnp.int32),
            pltpu.SMEM(tenant_ids.shape, jnp.int32),
            pltpu.VMEM((slot_count, KB, row_width), BF16),
            pltpu.VMEM((slot_count, row_width), BF16),
            pltpu.VMEM((RQ, out_weight.shape[1]), BF16),
            pltpu.VMEM((1, RQ), F32),
            pltpu.VMEM((1, RQ), F32),
            pltpu.VMEM(query_weight.shape, BF16),
            pltpu.VMEM(key_absorb.shape, BF16),
            pltpu.VMEM((2,) + value_up.shape[1:], BF16),
            pltpu.VMEM(out_weight.shape, BF16),
            pltpu.VMEM((RQ, row_width, BLK), BF16),
            pltpu.VMEM(head_weight.shape, BF16),
            pltpu.VMEM((seq_count, PAIR, NOPE + ROPE), BF16),
            pltpu.VMEM((H * RQ, row_width), BF16),
            pltpu.VMEM((RQ, KB, row_width), BF16),
            pltpu.VMEM((PAIR, row_width), BF16),
            pltpu.VMEM((RQ, MESSAGE, LANES), BF16),
            pltpu.VMEM((seq_count - 1, MESSAGE, LANES), BF16),
            pltpu.VMEM((seq_count, MESSAGE, LANES), BF16),
            pltpu.VMEM((seq_count, PAIR, LAT + 128), BF16),
            pltpu.VMEM((seq_count, PAIR, LAT + 128), BF16),
            pltpu.VMEM((seq_count, PAIR, VH), BF16),
            pltpu.VMEM((mp_count, seq_count, PAIR, out_weight.shape[1] // 2), BF16),
            pltpu.VMEM((seq_count * mp_count, 1, 128), F32),
            pltpu.SemaphoreType.DMA((13,)),
            pltpu.SemaphoreType.DMA((5,)),
        ]
        + [seq_sems] * 10
        + [mp_sems] * 2
        + [all_sems] * 2,
        compiler_params=pltpu.CompilerParams(
            collective_id=0, has_side_effects=True, vmem_limit_bytes=60 * 2**20
        ),
    )(
        hidden_in,
        keep_lists,
        drop_weights,
        final_gain,
        pack_dest,
        jnp.swapaxes(tenant_ranges, 0, 1),
        tenant_ids,
        query_weight,
        key_absorb,
        value_up,
        out_weight,
        jnp.swapaxes(latent_cache, 1, 2),
        head_weight,
    )
    outs = pl.pallas_call(
        publish_kernel,
        out_shape=tuple(jax.ShapeDtypeStruct(out.shape, out.dtype) for out in outs),
        in_specs=[hbm] * 5,
        out_specs=(hbm,) * 5,
        scratch_shapes=[pltpu.SemaphoreType.DMA((5,))],
        compiler_params=pltpu.CompilerParams(vmem_limit_bytes=60 * 2**20),
    )(*outs)
    packed_rows, packed_summary, hidden_out, state_norm, top_logit = outs
    return (
        packed_rows,
        packed_summary,
        hidden_out,
        state_norm.reshape(RQ),
        top_logit.reshape(RQ),
    )


def solution(mesh):
    in_specs = (
        P("mp", None),
        P(None, "seq"),
        P(),
        P(),
        P(None, "seq"),
        P("mp", "seq", None),
        P("mp"),
        P("mp", "seq", None),
        P("mp", "seq"),
        P("mp", None),
        P(),
        P(None, ("seq", "mp")),
        P(),
        P(),
    )
    out_specs = (
        P(("seq", "mp"), None, None),
        P(("seq", "mp"), None),
        P("mp", "seq"),
        P("mp"),
        P("mp"),
    )
    seq_count = mesh.shape["seq"]
    fused = seq_count * 2 == H
    return jax.shard_map(fused_body if fused else body, mesh=mesh, in_specs=in_specs, out_specs=out_specs, check_vma=False)
```

```python
import functools

import jax
import jax.numpy as jnp
from jax import lax
from jax.experimental import pallas as pl
from jax.experimental.pallas import tpu as pltpu
from jax.sharding import PartitionSpec as P

H = 16
NOPE = 128
ROPE = 64
LAT = 512
VH = 128
BLK = 128
KB = 64
TENANTS = 4
RQ = 8


NEGATIVE = -1e30
HIGHEST = lax.Precision.HIGHEST


def merged(x, axis, combine):
    everything = jax.tree.map(lambda part: lax.all_gather(part, axis), x)
    initial = jax.tree.map(lambda part: part[0], everything)

    def step(k, so_far):
        return combine(so_far, jax.tree.map(lambda part: part[k], everything))

    return lax.fori_loop(1, lax.axis_size(axis), step, initial)


def compact_blocks(block_rows, keep_onehot, weights_dropped):
    kept_rows = jnp.einsum(
        "nkt,ntc->nkc", keep_onehot, block_rows, preferred_element_type=jnp.float32
    ).astype(jnp.bfloat16)
    weight_mass = jnp.sum(weights_dropped.astype(jnp.float32), axis=1)
    summed = jnp.einsum(
        "nt,ntc->nc", weights_dropped, block_rows, preferred_element_type=jnp.float32
    )
    summary = (summed / weight_mass[:, None]).astype(jnp.bfloat16)
    return (kept_rows, summary)


def attend_blocks(query_lat, query_rope, kept_rows, summary, usable):
    score_scale = (NOPE + ROPE) ** (-0.5)
    row_scores = (
        jnp.einsum(
            "nhl,nkl->nhk", query_lat, kept_rows[:, :, :LAT], preferred_element_type=jnp.float32
        )
        + jnp.einsum(
            "nhr,nkr->nhk", query_rope, kept_rows[:, :, LAT:], preferred_element_type=jnp.float32
        )
    ) * score_scale
    summ_scores = (
        jnp.einsum("nhl,nl->nh", query_lat, summary[:, :LAT], preferred_element_type=jnp.float32)
        + jnp.einsum("nhr,nr->nh", query_rope, summary[:, LAT:], preferred_element_type=jnp.float32)
    ) * score_scale
    summ_scores = summ_scores + jnp.log(jnp.float32(BLK - KB))
    row_scores = jnp.where(usable[:, None, None], row_scores, NEGATIVE)
    summ_scores = jnp.where(usable[:, None], summ_scores, NEGATIVE)
    maxima = jnp.maximum(jnp.max(row_scores, axis=2), summ_scores)
    row_weights = jnp.where(usable[:, None, None], jnp.exp(row_scores - maxima[:, :, None]), 0.0)
    summ_weights = jnp.where(usable[:, None], jnp.exp(summ_scores - maxima), 0.0)
    totals = jnp.sum(row_weights, axis=2) + summ_weights
    weighted = jnp.einsum(
        "nhk,nkl->nhl", row_weights, kept_rows[:, :, :LAT].astype(jnp.float32), precision=HIGHEST
    )
    weighted = weighted + summ_weights[:, :, None] * summary[:, None, :LAT].astype(jnp.float32)
    return (maxima, totals, weighted)


def per_request(maxima, totals, weighted, owner_of):
    request_max = jnp.max(jnp.where(owner_of[:, :, None], maxima[None, :, :], NEGATIVE), axis=1)
    shifted = jnp.where(owner_of[:, :, None], maxima[None, :, :] - request_max[:, None, :], 0.0)
    factor = jnp.where(owner_of[:, :, None], jnp.exp(shifted), 0.0)
    request_total = jnp.einsum("rnh,nh->rh", factor, totals, precision=HIGHEST)
    request_sum = jnp.einsum("rnh,nhl->rhl", factor, weighted, precision=HIGHEST)
    return (request_max, request_total, request_sum)


def combine_partial(former, latter):
    former_max, former_total, former_sum = former
    latter_max, latter_total, latter_sum = latter
    joined = jnp.maximum(former_max, latter_max)
    former_factor = jnp.exp(former_max - joined)
    latter_factor = jnp.exp(latter_max - joined)
    return (
        joined,
        former_factor * former_total + latter_factor * latter_total,
        former_factor[:, :, None] * former_sum + latter_factor[:, :, None] * latter_sum,
    )


def body(
    hidden_in,
    query_weight,
    key_absorb,
    value_up,
    out_weight,
    latent_cache,
    cache_lengths,
    keep_lists,
    drop_weights,
    pack_dest,
    final_gain,
    head_weight,
    tenant_ranges,
    tenant_ids,
):
    seq_count = lax.axis_size("seq")
    mp_count = lax.axis_size("mp")
    seq_index = lax.axis_index("seq")
    mp_index = lax.axis_index("mp")
    capacity = max(1, RQ // seq_count)
    slot_count = RQ // 2
    row_width = LAT + ROPE
    query_part = jnp.dot(hidden_in, query_weight, preferred_element_type=jnp.float32).astype(
        jnp.bfloat16
    )
    query_full = lax.all_gather(query_part, "seq", axis=1, tiled=True).reshape(RQ, H, NOPE + ROPE)
    query_lat = jnp.einsum(
        "rhn,hnl->rhl", query_full[:, :, :NOPE], key_absorb, preferred_element_type=jnp.float32
    ).astype(jnp.bfloat16)
    query_rope = query_full[:, :, NOPE:]
    positions = jnp.arange(BLK, dtype=jnp.int32)
    keep_onehot = keep_lists[:, 0, :, None] == positions[None, None, :]
    kept_flag = jnp.sum(keep_onehot.astype(jnp.int32), axis=1)
    weights_dropped = (drop_weights * (1 - kept_flag)).astype(jnp.bfloat16)
    live_here = cache_lengths > seq_index * BLK
    dest_here = lax.dynamic_slice_in_dim(pack_dest, seq_index, 1, 1)[:, 0]
    send_slot = dest_here // slot_count * capacity + dest_here % slot_count % capacity
    slot_range = jnp.arange(seq_count * capacity, dtype=jnp.int32)
    send_onehot = ((send_slot[None, :] == slot_range[:, None]) & live_here[None, :]).astype(
        jnp.bfloat16
    )
    targets = seq_index * slot_count + jnp.arange(slot_count, dtype=jnp.int32)
    slot_match = (pack_dest[None, :, :] == targets[:, None, None]).astype(jnp.int32)
    block_range = jnp.arange(pack_dest.shape[1], dtype=jnp.int32)
    source_of = jnp.sum(slot_match * block_range[None, None, :], axis=(1, 2))
    request_of = jnp.sum(slot_match, axis=2)
    request_index = jnp.sum(request_of * jnp.arange(RQ, dtype=jnp.int32)[None, :], axis=1)
    pick_index = source_of * capacity + jnp.arange(slot_count, dtype=jnp.int32) % capacity
    owner_of = jnp.transpose(request_of) > 0
    local_rows, local_summary = compact_blocks(
        latent_cache, keep_onehot.astype(jnp.bfloat16), weights_dropped
    )
    send_rows = jnp.einsum(
        "jr,rkc->jkc", send_onehot, local_rows, preferred_element_type=jnp.float32
    )
    send_rows = send_rows.astype(jnp.bfloat16).reshape(seq_count, capacity, KB, row_width)
    send_summary = jnp.dot(send_onehot, local_summary, preferred_element_type=jnp.float32)
    send_summary = send_summary.astype(jnp.bfloat16).reshape(seq_count, capacity, row_width)
    recv_rows, recv_summary = (
        lax.all_to_all(send_rows, "seq", split_axis=0, concat_axis=0, tiled=True),
        lax.all_to_all(send_summary, "seq", split_axis=0, concat_axis=0, tiled=True),
    )
    packed_rows = jnp.take(
        recv_rows.reshape(seq_count * capacity, KB, row_width), pick_index, axis=0
    )
    packed_summary = jnp.take(
        recv_summary.reshape(seq_count * capacity, row_width), pick_index, axis=0
    )
    slot_query_lat = jnp.take(query_lat, request_index, axis=0)
    slot_query_rope = jnp.take(query_rope, request_index, axis=0)
    usable = jnp.ones((slot_count,), dtype=bool)
    maxima, totals, weighted = attend_blocks(
        slot_query_lat, slot_query_rope, packed_rows, packed_summary, usable
    )
    partial_value = per_request(maxima, totals, weighted, owner_of)
    request_max, request_total, request_sum = merged(partial_value, "seq", combine_partial)
    attended = (request_sum / request_total[:, :, None]).astype(jnp.bfloat16)
    values = jnp.einsum("rhl,hlv->rhv", attended, value_up, preferred_element_type=jnp.float32)
    values = values.astype(jnp.bfloat16).reshape(RQ, H * VH)
    col_width = out_weight.shape[1]
    residual = lax.dynamic_slice_in_dim(hidden_in, seq_index * col_width, col_width, 1)
    hidden_out = (
        residual.astype(jnp.float32)
        + jnp.dot(values, out_weight, preferred_element_type=jnp.float32)
    ).astype(jnp.bfloat16)
    gathered = lax.all_gather(hidden_out[None], ("seq", "mp"), axis=0, tiled=True)
    all_rows = gathered.reshape(seq_count, mp_count, RQ, col_width).transpose(1, 2, 0, 3)
    all_rows = all_rows.reshape(mp_count * RQ, seq_count * col_width)
    rows_f = all_rows.astype(jnp.float32)
    mean_sq = jnp.mean(rows_f * rows_f, axis=1)
    norms_all = jnp.sqrt(mean_sq)
    normed = (
        rows_f * lax.rsqrt(mean_sq + 1e-06)[:, None] * final_gain.astype(jnp.float32)[None, :]
    ).astype(jnp.bfloat16)
    logits = jnp.dot(normed, head_weight, preferred_element_type=jnp.float32)
    vocab_width = head_weight.shape[1]
    device_index = seq_index * mp_count + mp_index
    columns = device_index * vocab_width + jnp.arange(vocab_width, dtype=jnp.int32)
    tenant_onehot = (tenant_ids[:, None] == jnp.arange(TENANTS, dtype=jnp.int32)[None, :]).astype(
        jnp.int32
    )
    window_low = jnp.sum(tenant_onehot * tenant_ranges[None, :, 0], axis=1)
    window_high = jnp.sum(tenant_onehot * tenant_ranges[None, :, 1], axis=1)
    allowed = (columns[None, :] >= window_low[:, None]) & (columns[None, :] < window_high[:, None])
    local_best = jnp.max(jnp.where(allowed, logits, NEGATIVE), axis=1)
    best_all = lax.pmax(local_best, ("seq", "mp"))
    row_start = mp_index * RQ
    state_norm = lax.dynamic_slice_in_dim(norms_all, row_start, RQ, 0)
    top_logit = lax.dynamic_slice_in_dim(best_all, row_start, RQ, 0)
    return (packed_rows, packed_summary, hidden_out, state_norm, top_logit)


F32 = jnp.float32
BF16 = jnp.bfloat16
PAIR = 2 * RQ
LANES = 128
ROPE_AT = LAT // LANES * KB
SUMM_AT = ROPE_AT + KB // 2
MESSAGE = SUMM_AT + PAIR


def to_peer(src, dst, send_sem, recv_sem, device):
    copy = pltpu.make_async_remote_copy(
        src_ref=src,
        dst_ref=dst,
        send_sem=send_sem,
        recv_sem=recv_sem,
        device_id=device,
        device_id_type=pl.DeviceIdType.MESH,
    )
    copy.start()
    return copy


def as_row(column):
    wide = jnp.broadcast_to(column[:, :1], (RQ, RQ))
    sub = lax.broadcasted_iota(jnp.int32, (RQ, RQ), 0)
    lane = lax.broadcasted_iota(jnp.int32, (RQ, RQ), 1)
    return jnp.sum(jnp.where(sub == lane, wide, 0.0), axis=0, keepdims=True)


def unfold(part):
    wide = part.astype(F32)
    return jnp.concatenate([wide[:RQ], wide[RQ:]], axis=1)


def fold(x):
    width = x.shape[1] // 2
    return jnp.concatenate([x[:, :width], x[:, width:]], axis=0)


def layer_kernel(
    seq_count,
    mp_count,
    vocab_width,
    tile,
    hidden_hbm,
    keep_hbm,
    drop_hbm,
    gain_hbm,
    dest_hbm,
    ranges_hbm,
    ids_hbm,
    query_hbm,
    absorb_hbm,
    up_hbm,
    out_hbm,
    cache_hbm,
    head_hbm,
    rows_hbm,
    summary_hbm,
    hidden_out_hbm,
    norm_hbm,
    top_hbm,
    hidden_ref,
    keep_ref,
    drop_ref,
    gain_ref,
    dest_ref,
    ranges_ref,
    ids_ref,
    rows_out,
    summary_out,
    hidden_out,
    norm_out,
    top_out,
    query_w,
    absorb_w,
    up_w,
    out_w,
    cache,
    head_w,
    query_recv,
    query_flat,
    kept,
    summ,
    blocks,
    block_send,
    block_recv,
    part_send,
    part_recv,
    value_recv,
    hidden_all,
    best_all,
    local_sem,
    store_sem,
    q_send,
    q_recv,
    r_send,
    r_recv,
    p_send,
    p_recv,
    v_send,
    v_recv,
    h_send,
    h_recv,
    g_send,
    g_recv,
    b_send,
    b_recv,
):
    me = lax.axis_index("seq")
    my_mp = lax.axis_index("mp")
    slot_count = RQ // 2
    block_count = dest_ref.shape[1]
    row_width = LAT + ROPE
    contract = (((1,), (1,)), ((), ()))

    def seq_peer(k):
        return lax.rem(me + k, seq_count)

    def mp_peer(k):
        return lax.rem(my_mp + k, mp_count)

    def load(i, src, dst):
        copy = pltpu.make_async_copy(src, dst, local_sem.at[i])
        copy.start()
        return copy

    keep_load = load(0, keep_hbm, keep_ref)
    drop_load = load(1, drop_hbm, drop_ref)
    hidden_load = load(2, hidden_hbm, hidden_ref)
    query_load = load(3, query_hbm, query_w)
    dest_load = load(4, dest_hbm, dest_ref)
    cache_load = load(5, cache_hbm, cache)
    gain_load = load(6, gain_hbm, gain_ref)
    ranges_load = load(7, ranges_hbm, ranges_ref)
    ids_load = load(8, ids_hbm, ids_ref)
    absorb_load = load(9, absorb_hbm, absorb_w)

    def other(k):
        place = lax.rem(me * mp_count + my_mp + k, seq_count * mp_count)
        return (place // mp_count, lax.rem(place, mp_count))

    device_count = seq_count * mp_count
    barrier = pltpu.get_barrier_semaphore()
    for k in range(1, device_count):
        pl.semaphore_signal(
            barrier, inc=1, device_id=other(k), device_id_type=pl.DeviceIdType.MESH
        )
    keep_load.wait()
    drop_load.wait()

    keep = jnp.concatenate([keep_ref[:, 0, :], keep_ref[:, 0, :]], axis=1).astype(F32)
    keep_t = jnp.transpose(keep)[:KB]
    position = lax.broadcasted_iota(jnp.int32, (KB, BLK), 1).astype(F32)
    request_sub = lax.broadcasted_iota(jnp.int32, (RQ, BLK), 0)
    picks = []
    kept_flag = jnp.zeros((RQ, BLK), F32)
    for r in range(RQ):
        pick = jnp.where(jnp.broadcast_to(keep_t[:, r : r + 1], (KB, BLK)) == position, 1.0, 0.0)
        flag = jnp.sum(pick, axis=0, keepdims=True)
        kept_flag = jnp.where(request_sub == r, jnp.broadcast_to(flag, (RQ, BLK)), kept_flag)
        picks.append(pick)
    dropped = drop_ref[...].astype(F32) * (1.0 - kept_flag)
    mass = jnp.sum(dropped, axis=1, keepdims=True)

    hidden_load.wait()
    query_load.wait()
    query = jnp.dot(hidden_ref[...], query_w[...], preferred_element_type=F32)
    query_recv[me] = fold(query).astype(BF16)
    pl.semaphore_wait(barrier, device_count - 1)
    query_copies = [
        to_peer(
            query_recv.at[me],
            query_recv.at[me],
            q_send.at[k - 1],
            q_recv.at[k - 1],
            (seq_peer(k), my_mp),
        )
        for k in range(1, seq_count)
    ]
    out_load = load(10, out_hbm, out_w)
    up_load = load(11, up_hbm.at[pl.ds(me * 2, 2)], up_w)
    head_load = load(12, head_hbm, head_w)

    cache_load.wait()
    summed = jnp.zeros((PAIR, row_width), F32)
    pad = jnp.zeros((PAIR - RQ, BLK), F32)
    for r in range(RQ):
        own = jnp.where(request_sub == r, dropped, 0.0)
        both = jnp.concatenate([picks[r], own, pad], axis=0).astype(BF16)
        chosen = lax.dot_general(both, cache[r], contract, preferred_element_type=F32)
        summed = summed + chosen[KB:]
        chosen = chosen[:KB]
        kept[r] = chosen.astype(BF16)
        for i in range(LAT // LANES):
            piece = chosen[:, i * LANES : (i + 1) * LANES]
            blocks[r, i * KB : (i + 1) * KB, :] = piece.astype(BF16)
        rope = chosen[:, LAT:]
        rope = jnp.concatenate([rope[: KB // 2], rope[KB // 2 :]], axis=1)
        blocks[r, ROPE_AT:SUMM_AT, :] = rope.astype(BF16)
    mass_pair = jnp.concatenate([mass, jnp.ones_like(mass)], axis=0)
    summary = (summed / mass_pair).astype(BF16)
    summ[...] = summary
    summary_f = summary.astype(F32)[:RQ]
    summary_f = jnp.concatenate(
        [summary_f, jnp.zeros((RQ, 5 * LANES - row_width), F32)], axis=1
    )
    line = lax.broadcasted_iota(jnp.int32, (PAIR, LANES), 0)
    for r in range(RQ):
        lines = jnp.zeros((PAIR, LANES), F32)
        for i in range(5):
            piece = summary_f[r : r + 1, i * LANES : (i + 1) * LANES]
            lines = jnp.where(line == i, jnp.broadcast_to(piece, (PAIR, LANES)), lines)
        blocks[r, SUMM_AT:, :] = lines.astype(BF16)

    dest_load.wait()
    owners = [dest_ref[r, me] >> 2 for r in range(RQ)]

    def request_for(owner):
        chosen = jnp.int32(0)
        for r in range(RQ):
            chosen = jnp.where(owners[r] == owner, jnp.int32(r), chosen)
        return chosen

    block_recv[me] = blocks[request_for(me)]
    for k in range(1, seq_count):
        block_send[k - 1] = blocks[request_for(seq_peer(k))]

    def start_pack(k):
        return to_peer(
            block_send.at[k - 1],
            block_recv.at[me],
            r_send.at[k - 1],
            r_recv.at[k - 1],
            (seq_peer(k), my_mp),
        )

    far = seq_count // 2
    lots = ((far, 1, seq_count - 1), (2,), tuple(range(3, far)) + tuple(range(far + 1, seq_count - 1)))
    pack_copies = [start_pack(k) for k in lots[0]]

    absorb_load.wait()
    for copy in query_copies:
        copy.wait_recv()
    first_half = lax.broadcasted_iota(jnp.int32, (PAIR, NOPE), 0) < RQ
    for s in range(seq_count):
        part = query_recv[s]
        nope = part[:, :NOPE].astype(F32)
        split = jnp.concatenate(
            [jnp.where(first_half, nope, 0.0), jnp.where(first_half, 0.0, nope)], axis=1
        ).astype(BF16)
        weight = absorb_w[2 * s : 2 * s + 2].reshape(2 * NOPE, LAT)
        latent = jnp.dot(split, weight, preferred_element_type=F32).astype(BF16)
        query_flat[PAIR * s : PAIR * (s + 1), :LAT] = latent
        query_flat[PAIR * s : PAIR * (s + 1), LAT:] = part[:, NOPE:]

    rows = H * RQ
    score_scale = (NOPE + ROPE) ** (-0.5)
    flat = query_flat[...]
    kept_all = kept[...].reshape(RQ * KB, row_width)
    row_scores = lax.dot_general(flat, kept_all, contract, preferred_element_type=F32)
    summ_scores = lax.dot_general(flat, summ[...], contract, preferred_element_type=F32)
    row_request = lax.broadcasted_iota(jnp.int32, (rows, RQ * KB), 0) & (RQ - 1)
    col_request = lax.broadcasted_iota(jnp.int32, (rows, RQ * KB), 1) // KB
    row_scores = jnp.where(row_request == col_request, row_scores * score_scale, NEGATIVE)
    summ_request = lax.broadcasted_iota(jnp.int32, (rows, PAIR), 0) & (RQ - 1)
    summ_column = lax.broadcasted_iota(jnp.int32, (rows, PAIR), 1)
    summ_scores = summ_scores * score_scale + jnp.log(F32(BLK - KB))
    summ_scores = jnp.where(summ_request == summ_column, summ_scores, NEGATIVE)
    maxima = jnp.maximum(
        jnp.max(row_scores, axis=1, keepdims=True), jnp.max(summ_scores, axis=1, keepdims=True)
    )
    row_weights = jnp.exp(row_scores - maxima)
    summ_weights = jnp.exp(summ_scores - maxima)
    totals = jnp.sum(row_weights, axis=1, keepdims=True) + jnp.sum(
        summ_weights, axis=1, keepdims=True
    )
    weighted = jnp.dot(
        row_weights.astype(BF16), kept_all[:, :LAT], preferred_element_type=F32
    ) + jnp.dot(summ_weights.astype(BF16), summ[:, :LAT], preferred_element_type=F32)
    live_rows = lax.broadcasted_iota(jnp.int32, (rows, 128), 0) & (RQ - 1)
    level = jnp.broadcast_to(maxima + jnp.log(totals), (rows, 128))
    for r in range(RQ):
        level = jnp.where((live_rows == r) & (owners[r] < 0), NEGATIVE, level)
    high = level.astype(BF16).astype(F32)
    middle = (level - high).astype(BF16).astype(F32)
    low = level - high - middle
    lane = lax.broadcasted_iota(jnp.int32, (rows, 128), 1)
    terms = jnp.where(
        lane == 0, high, jnp.where(lane == 1, middle, jnp.where(lane == 2, low, 0.0))
    )
    part_send[:, :, :LAT] = (weighted / totals).astype(BF16).reshape(seq_count, PAIR, LAT)
    part_send[:, :, LAT:] = terms.astype(BF16).reshape(seq_count, PAIR, 128)
    part_copies = [
        to_peer(
            part_send.at[seq_peer(k)],
            part_recv.at[me],
            p_send.at[k - 1],
            p_recv.at[k - 1],
            (seq_peer(k), my_mp),
        )
        for k in range(1, seq_count)
    ]
    part_recv[me] = part_send[me]

    ranges_load.wait()
    ids_load.wait()
    total_rows = mp_count * RQ
    window_row = lax.broadcasted_iota(jnp.int32, (total_rows, 128), 0)
    window_low = jnp.zeros((total_rows, 128), jnp.int32)
    window_high = jnp.zeros((total_rows, 128), jnp.int32)
    for row in range(total_rows):
        tenant = ids_ref[row]
        window_low = jnp.where(window_row == row, ranges_ref[0, tenant], window_low)
        window_high = jnp.where(window_row == row, ranges_ref[1, tenant], window_high)
    vocab_start = (me * mp_count + my_mp) * vocab_width
    window_low = window_low - vocab_start
    window_high = window_high - vocab_start

    slot_source = [jnp.int32(0)] * slot_count
    for r in range(RQ):
        for b in range(block_count):
            offset = dest_ref[r, b] - me * slot_count
            for j in range(slot_count):
                slot_source[j] = jnp.where(offset == j, jnp.int32(b), slot_source[j])

    up_load.wait()
    for copy in part_copies:
        copy.wait_recv()
    pack_copies += [start_pack(k) for k in lots[1]]
    levels = [
        jnp.sum(part_recv[s, :, LAT:].astype(F32), axis=1, keepdims=True)
        for s in range(seq_count)
    ]
    peak = functools.reduce(jnp.maximum, levels)
    factors = [jnp.exp(part_level - peak) for part_level in levels]
    merged_sum = functools.reduce(
        jnp.add, [factors[s] * part_recv[s, :, :LAT].astype(F32) for s in range(seq_count)]
    )
    attended = (merged_sum / functools.reduce(jnp.add, factors)).astype(BF16).astype(F32)
    first_wide = lax.broadcasted_iota(jnp.int32, (PAIR, LAT), 0) < RQ
    split = jnp.concatenate(
        [jnp.where(first_wide, attended, 0.0), jnp.where(first_wide, 0.0, attended)], axis=1
    ).astype(BF16)
    values = jnp.dot(split, up_w[...].reshape(2 * LAT, VH), preferred_element_type=F32)
    value_recv[me] = values.astype(BF16)
    value_copies = [
        to_peer(
            value_recv.at[me],
            value_recv.at[me],
            v_send.at[k - 1],
            v_recv.at[k - 1],
            (seq_peer(k), my_mp),
        )
        for k in range(1, seq_count)
    ]
    out_load.wait()
    for copy in value_copies:
        copy.wait_recv()
    all_values = jnp.concatenate(
        [unfold(value_recv[s]) for s in range(seq_count)], axis=1
    ).astype(BF16)
    col_width = out_w.shape[1]
    residual = hidden_ref[:, pl.ds(pl.multiple_of(me * col_width, 128), col_width)]
    hidden = residual.astype(F32) + jnp.dot(all_values, out_w[...], preferred_element_type=F32)
    hidden = hidden.astype(BF16)
    hidden_out[...] = hidden

    def store(i, src, dst):
        copy = pltpu.make_async_copy(src, dst, store_sem.at[i])
        copy.start()
        return copy

    stores = [store(0, hidden_out, hidden_out_hbm)]
    hidden_all[my_mp, me] = fold(hidden.astype(F32)).astype(BF16)

    hidden_copies = [
        to_peer(
            hidden_all.at[my_mp, me],
            hidden_all.at[my_mp, me],
            h_send.at[k - 1],
            h_recv.at[k - 1],
            (seq_peer(k), my_mp),
        )
        for k in range(1, seq_count)
    ]
    for copy in hidden_copies:
        copy.wait_recv()
    group_copies = [
        to_peer(
            hidden_all.at[my_mp],
            hidden_all.at[my_mp],
            g_send.at[k - 1],
            g_recv.at[k - 1],
            (me, mp_peer(k)),
        )
        for k in range(1, mp_count)
    ]
    own_rows = jnp.concatenate(
        [unfold(hidden_all[my_mp, s]) for s in range(seq_count)], axis=1
    )
    own_norm = jnp.sqrt(jnp.mean(own_rows * own_rows, axis=1, keepdims=True))
    norm_out[...] = as_row(own_norm)
    stores.append(store(1, norm_out, norm_hbm))
    gain_load.wait()
    gain = gain_ref[...].astype(F32).reshape(1, -1)
    for copy in group_copies:
        copy.wait_recv()
    pack_copies += [start_pack(k) for k in lots[2]]
    normed = []
    for m in range(mp_count):
        group = jnp.concatenate([unfold(hidden_all[m, s]) for s in range(seq_count)], axis=1)
        mean_sq = jnp.mean(group * group, axis=1, keepdims=True)
        normed.append(group * lax.rsqrt(mean_sq + 1e-06) * gain)
    normed = jnp.concatenate(normed, axis=0).astype(BF16)

    head_load.wait()
    lane = lax.broadcasted_iota(jnp.int32, (total_rows, 128), 1)

    def head_step(n, best):
        start = pl.multiple_of(n * tile, 128)
        logits = jnp.dot(normed, head_w[:, pl.ds(start, tile)], preferred_element_type=F32)
        for i in range(tile // 128):
            column = lane + (start + i * 128)
            allowed = (column >= window_low) & (column < window_high)
            best = jnp.maximum(
                best, jnp.where(allowed, logits[:, i * 128 : (i + 1) * 128], NEGATIVE)
            )
        return best

    best = lax.fori_loop(
        0, vocab_width // tile, head_step, jnp.full((total_rows, 128), NEGATIVE, F32)
    )
    best = jnp.broadcast_to(jnp.max(best, axis=1, keepdims=True), (total_rows, 128))
    diagonal = window_row == lane
    here = me * mp_count + my_mp
    best_all[here] = jnp.sum(jnp.where(diagonal, best, 0.0), axis=0, keepdims=True)
    best_copies = [
        to_peer(
            best_all.at[here], best_all.at[here], b_send.at[k - 1], b_recv.at[k - 1], other(k)
        )
        for k in range(1, device_count)
    ]

    for copy in pack_copies:
        copy.wait_recv()
    lines = []
    for j in range(slot_count):
        source = slot_source[j]
        block = block_recv[source]
        for i in range(LAT // LANES):
            rows_out[j, :, i * LANES : (i + 1) * LANES] = block[i * KB : (i + 1) * KB]
        rope = block[ROPE_AT:SUMM_AT].astype(F32)
        rope = jnp.concatenate([rope[:, :ROPE], rope[:, ROPE:]], axis=0)
        rows_out[j, :, LAT:] = rope.astype(BF16)
        tail = block[SUMM_AT:].astype(F32)
        line = jnp.concatenate([tail[i : i + 1] for i in range(5)], axis=1)
        lines.append(line[:, :row_width])
    summary_out[...] = jnp.concatenate(lines, axis=0).astype(BF16)
    stores.append(store(2, rows_out, rows_hbm))
    stores.append(store(3, summary_out, summary_hbm))

    for copy in best_copies:
        copy.wait_recv()
    top = jnp.max(best_all[...], axis=0)
    own_top = top[:, :RQ]
    for m in range(1, mp_count):
        own_top = jnp.where(my_mp == m, top[:, m * RQ : (m + 1) * RQ], own_top)
    top_out[...] = own_top
    stores.append(store(4, top_out, top_hbm))
    for copy in (
        query_copies
        + pack_copies
        + part_copies
        + value_copies
        + hidden_copies
        + group_copies
        + best_copies
    ):
        copy.wait_send()
    for copy in stores:
        copy.wait()


def publish_kernel(*refs):
    results, places, staged = refs[:5], refs[5:10], refs[10:15]
    in_sem, out_sem = refs[15:]
    loads = [
        pltpu.make_async_copy(result, stage, in_sem.at[i])
        for i, (result, stage) in enumerate(zip(results, staged))
    ]
    stores = [
        pltpu.make_async_copy(stage, place, out_sem.at[i])
        for i, (stage, place) in enumerate(zip(staged, places))
    ]
    for copy in loads:
        copy.start()
    for load, store in zip(loads, stores):
        load.wait()
        store.start()
    for copy in stores:
        copy.wait()


def fused_body(
    hidden_in,
    query_weight,
    key_absorb,
    value_up,
    out_weight,
    latent_cache,
    cache_lengths,
    keep_lists,
    drop_weights,
    pack_dest,
    final_gain,
    head_weight,
    tenant_ranges,
    tenant_ids,
):
    seq_count = lax.axis_size("seq")
    mp_count = lax.axis_size("mp")
    row_width = LAT + ROPE
    slot_count = RQ // 2
    depth, vocab_width = head_weight.shape
    tile = next(t for t in (640, 512, 384, 256, 128) if vocab_width % t == 0)
    hbm = pl.BlockSpec(memory_space=pltpu.HBM)
    seq_sems = pltpu.SemaphoreType.DMA((seq_count - 1,))
    all_sems = pltpu.SemaphoreType.DMA((seq_count * mp_count - 1,))
    mp_sems = pltpu.SemaphoreType.DMA((mp_count - 1,))
    outs = pl.pallas_call(
        functools.partial(layer_kernel, seq_count, mp_count, vocab_width, tile),
        out_shape=(
            jax.ShapeDtypeStruct((slot_count, KB, row_width), BF16),
            jax.ShapeDtypeStruct((slot_count, row_width), BF16),
            jax.ShapeDtypeStruct((RQ, out_weight.shape[1]), BF16),
            jax.ShapeDtypeStruct((1, RQ), F32),
            jax.ShapeDtypeStruct((1, RQ), F32),
        ),
        in_specs=[hbm] * 13,
        out_specs=(hbm,) * 5,
        scratch_shapes=[
            pltpu.VMEM(hidden_in.shape, BF16),
            pltpu.VMEM(keep_lists.shape, jnp.int32),
            pltpu.VMEM(drop_weights.shape, jnp.int32),
            pltpu.VMEM(final_gain.shape, BF16),
            pltpu.SMEM(pack_dest.shape, jnp.int32),
            pltpu.SMEM((2, TENANTS), jnp.int32),
            pltpu.SMEM(tenant_ids.shape, jnp.int32),
            pltpu.VMEM((slot_count, KB, row_width), BF16),
            pltpu.VMEM((slot_count, row_width), BF16),
            pltpu.VMEM((RQ, out_weight.shape[1]), BF16),
            pltpu.VMEM((1, RQ), F32),
            pltpu.VMEM((1, RQ), F32),
            pltpu.VMEM(query_weight.shape, BF16),
            pltpu.VMEM(key_absorb.shape, BF16),
            pltpu.VMEM((2,) + value_up.shape[1:], BF16),
            pltpu.VMEM(out_weight.shape, BF16),
            pltpu.VMEM((RQ, row_width, BLK), BF16),
            pltpu.VMEM(head_weight.shape, BF16),
            pltpu.VMEM((seq_count, PAIR, NOPE + ROPE), BF16),
            pltpu.VMEM((H * RQ, row_width), BF16),
            pltpu.VMEM((RQ, KB, row_width), BF16),
            pltpu.VMEM((PAIR, row_width), BF16),
            pltpu.VMEM((RQ, MESSAGE, LANES), BF16),
            pltpu.VMEM((seq_count - 1, MESSAGE, LANES), BF16),
            pltpu.VMEM((seq_count, MESSAGE, LANES), BF16),
            pltpu.VMEM((seq_count, PAIR, LAT + 128), BF16),
            pltpu.VMEM((seq_count, PAIR, LAT + 128), BF16),
            pltpu.VMEM((seq_count, PAIR, VH), BF16),
            pltpu.VMEM((mp_count, seq_count, PAIR, out_weight.shape[1] // 2), BF16),
            pltpu.VMEM((seq_count * mp_count, 1, 128), F32),
            pltpu.SemaphoreType.DMA((13,)),
            pltpu.SemaphoreType.DMA((5,)),
        ]
        + [seq_sems] * 10
        + [mp_sems] * 2
        + [all_sems] * 2,
        compiler_params=pltpu.CompilerParams(
            collective_id=0, has_side_effects=True, vmem_limit_bytes=60 * 2**20
        ),
    )(
        hidden_in,
        keep_lists,
        drop_weights,
        final_gain,
        pack_dest,
        jnp.swapaxes(tenant_ranges, 0, 1),
        tenant_ids,
        query_weight,
        key_absorb,
        value_up,
        out_weight,
        jnp.swapaxes(latent_cache, 1, 2),
        head_weight,
    )
    outs = pl.pallas_call(
        publish_kernel,
        out_shape=tuple(jax.ShapeDtypeStruct(out.shape, out.dtype) for out in outs),
        in_specs=[hbm] * 5,
        out_specs=(hbm,) * 5,
        scratch_shapes=[pltpu.VMEM(out.shape, out.dtype) for out in outs]
        + [pltpu.SemaphoreType.DMA((5,))] * 2,
        compiler_params=pltpu.CompilerParams(vmem_limit_bytes=60 * 2**20),
    )(*outs)
    packed_rows, packed_summary, hidden_out, state_norm, top_logit = outs
    return (
        packed_rows,
        packed_summary,
        hidden_out,
        state_norm.reshape(RQ),
        top_logit.reshape(RQ),
    )


def solution(mesh):
    in_specs = (
        P("mp", None),
        P(None, "seq"),
        P(),
        P(),
        P(None, "seq"),
        P("mp", "seq", None),
        P("mp"),
        P("mp", "seq", None),
        P("mp", "seq"),
        P("mp", None),
        P(),
        P(None, ("seq", "mp")),
        P(),
        P(),
    )
    out_specs = (
        P(("seq", "mp"), None, None),
        P(("seq", "mp"), None),
        P("mp", "seq"),
        P("mp"),
        P("mp"),
    )
    seq_count = mesh.shape["seq"]
    fused = seq_count * 2 == H
    return jax.shard_map(fused_body if fused else body, mesh=mesh, in_specs=in_specs, out_specs=out_specs, check_vma=False)
```

```python
import functools

import jax
import jax.numpy as jnp
from jax import lax
from jax.experimental import pallas as pl
from jax.experimental.pallas import tpu as pltpu
from jax.sharding import PartitionSpec as P

H = 16
NOPE = 128
ROPE = 64
LAT = 512
VH = 128
BLK = 128
KB = 64
TENANTS = 4
RQ = 8


NEGATIVE = -1e30
HIGHEST = lax.Precision.HIGHEST


def merged(x, axis, combine):
    everything = jax.tree.map(lambda part: lax.all_gather(part, axis), x)
    initial = jax.tree.map(lambda part: part[0], everything)

    def step(k, so_far):
        return combine(so_far, jax.tree.map(lambda part: part[k], everything))

    return lax.fori_loop(1, lax.axis_size(axis), step, initial)


def compact_blocks(block_rows, keep_onehot, weights_dropped):
    kept_rows = jnp.einsum(
        "nkt,ntc->nkc", keep_onehot, block_rows, preferred_element_type=jnp.float32
    ).astype(jnp.bfloat16)
    weight_mass = jnp.sum(weights_dropped.astype(jnp.float32), axis=1)
    summed = jnp.einsum(
        "nt,ntc->nc", weights_dropped, block_rows, preferred_element_type=jnp.float32
    )
    summary = (summed / weight_mass[:, None]).astype(jnp.bfloat16)
    return (kept_rows, summary)


def attend_blocks(query_lat, query_rope, kept_rows, summary, usable):
    score_scale = (NOPE + ROPE) ** (-0.5)
    row_scores = (
        jnp.einsum(
            "nhl,nkl->nhk", query_lat, kept_rows[:, :, :LAT], preferred_element_type=jnp.float32
        )
        + jnp.einsum(
            "nhr,nkr->nhk", query_rope, kept_rows[:, :, LAT:], preferred_element_type=jnp.float32
        )
    ) * score_scale
    summ_scores = (
        jnp.einsum("nhl,nl->nh", query_lat, summary[:, :LAT], preferred_element_type=jnp.float32)
        + jnp.einsum("nhr,nr->nh", query_rope, summary[:, LAT:], preferred_element_type=jnp.float32)
    ) * score_scale
    summ_scores = summ_scores + jnp.log(jnp.float32(BLK - KB))
    row_scores = jnp.where(usable[:, None, None], row_scores, NEGATIVE)
    summ_scores = jnp.where(usable[:, None], summ_scores, NEGATIVE)
    maxima = jnp.maximum(jnp.max(row_scores, axis=2), summ_scores)
    row_weights = jnp.where(usable[:, None, None], jnp.exp(row_scores - maxima[:, :, None]), 0.0)
    summ_weights = jnp.where(usable[:, None], jnp.exp(summ_scores - maxima), 0.0)
    totals = jnp.sum(row_weights, axis=2) + summ_weights
    weighted = jnp.einsum(
        "nhk,nkl->nhl", row_weights, kept_rows[:, :, :LAT].astype(jnp.float32), precision=HIGHEST
    )
    weighted = weighted + summ_weights[:, :, None] * summary[:, None, :LAT].astype(jnp.float32)
    return (maxima, totals, weighted)


def per_request(maxima, totals, weighted, owner_of):
    request_max = jnp.max(jnp.where(owner_of[:, :, None], maxima[None, :, :], NEGATIVE), axis=1)
    shifted = jnp.where(owner_of[:, :, None], maxima[None, :, :] - request_max[:, None, :], 0.0)
    factor = jnp.where(owner_of[:, :, None], jnp.exp(shifted), 0.0)
    request_total = jnp.einsum("rnh,nh->rh", factor, totals, precision=HIGHEST)
    request_sum = jnp.einsum("rnh,nhl->rhl", factor, weighted, precision=HIGHEST)
    return (request_max, request_total, request_sum)


def combine_partial(former, latter):
    former_max, former_total, former_sum = former
    latter_max, latter_total, latter_sum = latter
    joined = jnp.maximum(former_max, latter_max)
    former_factor = jnp.exp(former_max - joined)
    latter_factor = jnp.exp(latter_max - joined)
    return (
        joined,
        former_factor * former_total + latter_factor * latter_total,
        former_factor[:, :, None] * former_sum + latter_factor[:, :, None] * latter_sum,
    )


def body(
    hidden_in,
    query_weight,
    key_absorb,
    value_up,
    out_weight,
    latent_cache,
    cache_lengths,
    keep_lists,
    drop_weights,
    pack_dest,
    final_gain,
    head_weight,
    tenant_ranges,
    tenant_ids,
):
    seq_count = lax.axis_size("seq")
    mp_count = lax.axis_size("mp")
    seq_index = lax.axis_index("seq")
    mp_index = lax.axis_index("mp")
    capacity = max(1, RQ // seq_count)
    slot_count = RQ // 2
    row_width = LAT + ROPE
    query_part = jnp.dot(hidden_in, query_weight, preferred_element_type=jnp.float32).astype(
        jnp.bfloat16
    )
    query_full = lax.all_gather(query_part, "seq", axis=1, tiled=True).reshape(RQ, H, NOPE + ROPE)
    query_lat = jnp.einsum(
        "rhn,hnl->rhl", query_full[:, :, :NOPE], key_absorb, preferred_element_type=jnp.float32
    ).astype(jnp.bfloat16)
    query_rope = query_full[:, :, NOPE:]
    positions = jnp.arange(BLK, dtype=jnp.int32)
    keep_onehot = keep_lists[:, 0, :, None] == positions[None, None, :]
    kept_flag = jnp.sum(keep_onehot.astype(jnp.int32), axis=1)
    weights_dropped = (drop_weights * (1 - kept_flag)).astype(jnp.bfloat16)
    live_here = cache_lengths > seq_index * BLK
    dest_here = lax.dynamic_slice_in_dim(pack_dest, seq_index, 1, 1)[:, 0]
    send_slot = dest_here // slot_count * capacity + dest_here % slot_count % capacity
    slot_range = jnp.arange(seq_count * capacity, dtype=jnp.int32)
    send_onehot = ((send_slot[None, :] == slot_range[:, None]) & live_here[None, :]).astype(
        jnp.bfloat16
    )
    targets = seq_index * slot_count + jnp.arange(slot_count, dtype=jnp.int32)
    slot_match = (pack_dest[None, :, :] == targets[:, None, None]).astype(jnp.int32)
    block_range = jnp.arange(pack_dest.shape[1], dtype=jnp.int32)
    source_of = jnp.sum(slot_match * block_range[None, None, :], axis=(1, 2))
    request_of = jnp.sum(slot_match, axis=2)
    request_index = jnp.sum(request_of * jnp.arange(RQ, dtype=jnp.int32)[None, :], axis=1)
    pick_index = source_of * capacity + jnp.arange(slot_count, dtype=jnp.int32) % capacity
    owner_of = jnp.transpose(request_of) > 0
    local_rows, local_summary = compact_blocks(
        latent_cache, keep_onehot.astype(jnp.bfloat16), weights_dropped
    )
    send_rows = jnp.einsum(
        "jr,rkc->jkc", send_onehot, local_rows, preferred_element_type=jnp.float32
    )
    send_rows = send_rows.astype(jnp.bfloat16).reshape(seq_count, capacity, KB, row_width)
    send_summary = jnp.dot(send_onehot, local_summary, preferred_element_type=jnp.float32)
    send_summary = send_summary.astype(jnp.bfloat16).reshape(seq_count, capacity, row_width)
    recv_rows, recv_summary = (
        lax.all_to_all(send_rows, "seq", split_axis=0, concat_axis=0, tiled=True),
        lax.all_to_all(send_summary, "seq", split_axis=0, concat_axis=0, tiled=True),
    )
    packed_rows = jnp.take(
        recv_rows.reshape(seq_count * capacity, KB, row_width), pick_index, axis=0
    )
    packed_summary = jnp.take(
        recv_summary.reshape(seq_count * capacity, row_width), pick_index, axis=0
    )
    slot_query_lat = jnp.take(query_lat, request_index, axis=0)
    slot_query_rope = jnp.take(query_rope, request_index, axis=0)
    usable = jnp.ones((slot_count,), dtype=bool)
    maxima, totals, weighted = attend_blocks(
        slot_query_lat, slot_query_rope, packed_rows, packed_summary, usable
    )
    partial_value = per_request(maxima, totals, weighted, owner_of)
    request_max, request_total, request_sum = merged(partial_value, "seq", combine_partial)
    attended = (request_sum / request_total[:, :, None]).astype(jnp.bfloat16)
    values = jnp.einsum("rhl,hlv->rhv", attended, value_up, preferred_element_type=jnp.float32)
    values = values.astype(jnp.bfloat16).reshape(RQ, H * VH)
    col_width = out_weight.shape[1]
    residual = lax.dynamic_slice_in_dim(hidden_in, seq_index * col_width, col_width, 1)
    hidden_out = (
        residual.astype(jnp.float32)
        + jnp.dot(values, out_weight, preferred_element_type=jnp.float32)
    ).astype(jnp.bfloat16)
    gathered = lax.all_gather(hidden_out[None], ("seq", "mp"), axis=0, tiled=True)
    all_rows = gathered.reshape(seq_count, mp_count, RQ, col_width).transpose(1, 2, 0, 3)
    all_rows = all_rows.reshape(mp_count * RQ, seq_count * col_width)
    rows_f = all_rows.astype(jnp.float32)
    mean_sq = jnp.mean(rows_f * rows_f, axis=1)
    norms_all = jnp.sqrt(mean_sq)
    normed = (
        rows_f * lax.rsqrt(mean_sq + 1e-06)[:, None] * final_gain.astype(jnp.float32)[None, :]
    ).astype(jnp.bfloat16)
    logits = jnp.dot(normed, head_weight, preferred_element_type=jnp.float32)
    vocab_width = head_weight.shape[1]
    device_index = seq_index * mp_count + mp_index
    columns = device_index * vocab_width + jnp.arange(vocab_width, dtype=jnp.int32)
    tenant_onehot = (tenant_ids[:, None] == jnp.arange(TENANTS, dtype=jnp.int32)[None, :]).astype(
        jnp.int32
    )
    window_low = jnp.sum(tenant_onehot * tenant_ranges[None, :, 0], axis=1)
    window_high = jnp.sum(tenant_onehot * tenant_ranges[None, :, 1], axis=1)
    allowed = (columns[None, :] >= window_low[:, None]) & (columns[None, :] < window_high[:, None])
    local_best = jnp.max(jnp.where(allowed, logits, NEGATIVE), axis=1)
    best_all = lax.pmax(local_best, ("seq", "mp"))
    row_start = mp_index * RQ
    state_norm = lax.dynamic_slice_in_dim(norms_all, row_start, RQ, 0)
    top_logit = lax.dynamic_slice_in_dim(best_all, row_start, RQ, 0)
    return (packed_rows, packed_summary, hidden_out, state_norm, top_logit)


F32 = jnp.float32
BF16 = jnp.bfloat16
PAIR = 2 * RQ
LANES = 128
ROPE_AT = LAT // LANES * KB
SUMM_AT = ROPE_AT + KB // 2
MESSAGE = SUMM_AT + PAIR


def to_peer(src, dst, send_sem, recv_sem, device):
    copy = pltpu.make_async_remote_copy(
        src_ref=src,
        dst_ref=dst,
        send_sem=send_sem,
        recv_sem=recv_sem,
        device_id=device,
        device_id_type=pl.DeviceIdType.MESH,
    )
    copy.start()
    return copy


def as_row(column):
    wide = jnp.broadcast_to(column[:, :1], (RQ, RQ))
    sub = lax.broadcasted_iota(jnp.int32, (RQ, RQ), 0)
    lane = lax.broadcasted_iota(jnp.int32, (RQ, RQ), 1)
    return jnp.sum(jnp.where(sub == lane, wide, 0.0), axis=0, keepdims=True)


def unfold(part):
    wide = part.astype(F32)
    return jnp.concatenate([wide[:RQ], wide[RQ:]], axis=1)


def fold(x):
    width = x.shape[1] // 2
    return jnp.concatenate([x[:, :width], x[:, width:]], axis=0)


def layer_kernel(
    seq_count,
    mp_count,
    vocab_width,
    tile,
    hidden_hbm,
    keep_hbm,
    drop_hbm,
    gain_hbm,
    dest_hbm,
    ranges_hbm,
    ids_hbm,
    query_hbm,
    absorb_hbm,
    up_hbm,
    out_hbm,
    cache_hbm,
    head_hbm,
    rows_hbm,
    summary_hbm,
    hidden_out_hbm,
    norm_hbm,
    top_hbm,
    hidden_ref,
    keep_ref,
    drop_ref,
    gain_ref,
    dest_ref,
    ranges_ref,
    ids_ref,
    rows_out,
    summary_out,
    hidden_out,
    norm_out,
    top_out,
    query_w,
    absorb_w,
    up_w,
    out_w,
    cache,
    head_w,
    query_recv,
    query_flat,
    kept,
    summ,
    blocks,
    block_send,
    block_recv,
    part_send,
    part_recv,
    value_recv,
    hidden_all,
    best_all,
    local_sem,
    store_sem,
    q_send,
    q_recv,
    r_send,
    r_recv,
    p_send,
    p_recv,
    v_send,
    v_recv,
    h_send,
    h_recv,
    g_send,
    g_recv,
    b_send,
    b_recv,
):
    me = lax.axis_index("seq")
    my_mp = lax.axis_index("mp")
    slot_count = RQ // 2
    block_count = dest_ref.shape[1]
    row_width = LAT + ROPE
    contract = (((1,), (1,)), ((), ()))

    def seq_peer(k):
        return lax.rem(me + k, seq_count)

    def mp_peer(k):
        return lax.rem(my_mp + k, mp_count)

    def load(i, src, dst):
        copy = pltpu.make_async_copy(src, dst, local_sem.at[i])
        copy.start()
        return copy

    keep_load = load(0, keep_hbm, keep_ref)
    drop_load = load(1, drop_hbm, drop_ref)
    hidden_load = load(2, hidden_hbm, hidden_ref)
    query_load = load(3, query_hbm, query_w)
    dest_load = load(4, dest_hbm, dest_ref)
    cache_load = load(5, cache_hbm, cache)
    gain_load = load(6, gain_hbm, gain_ref)
    ranges_load = load(7, ranges_hbm, ranges_ref)
    ids_load = load(8, ids_hbm, ids_ref)
    absorb_load = load(9, absorb_hbm, absorb_w)

    def other(k):
        place = lax.rem(me * mp_count + my_mp + k, seq_count * mp_count)
        return (place // mp_count, lax.rem(place, mp_count))

    device_count = seq_count * mp_count
    barrier = pltpu.get_barrier_semaphore()
    for k in range(1, device_count):
        pl.semaphore_signal(
            barrier, inc=1, device_id=other(k), device_id_type=pl.DeviceIdType.MESH
        )
    keep_load.wait()
    drop_load.wait()

    keep = jnp.concatenate([keep_ref[:, 0, :], keep_ref[:, 0, :]], axis=1).astype(F32)
    keep_t = jnp.transpose(keep)[:KB]
    position = lax.broadcasted_iota(jnp.int32, (KB, BLK), 1).astype(F32)
    request_sub = lax.broadcasted_iota(jnp.int32, (RQ, BLK), 0)
    picks = []
    kept_flag = jnp.zeros((RQ, BLK), F32)
    for r in range(RQ):
        pick = jnp.where(jnp.broadcast_to(keep_t[:, r : r + 1], (KB, BLK)) == position, 1.0, 0.0)
        flag = jnp.sum(pick, axis=0, keepdims=True)
        kept_flag = jnp.where(request_sub == r, jnp.broadcast_to(flag, (RQ, BLK)), kept_flag)
        picks.append(pick)
    dropped = drop_ref[...].astype(F32) * (1.0 - kept_flag)
    mass = jnp.sum(dropped, axis=1, keepdims=True)

    hidden_load.wait()
    query_load.wait()
    query = jnp.dot(hidden_ref[...], query_w[...], preferred_element_type=F32)
    query_recv[me] = fold(query).astype(BF16)
    pl.semaphore_wait(barrier, device_count - 1)
    query_copies = [
        to_peer(
            query_recv.at[me],
            query_recv.at[me],
            q_send.at[k - 1],
            q_recv.at[k - 1],
            (seq_peer(k), my_mp),
        )
        for k in range(1, seq_count)
    ]
    out_load = load(10, out_hbm, out_w)
    up_load = load(11, up_hbm.at[pl.ds(me * 2, 2)], up_w)
    head_load = load(12, head_hbm, head_w)

    cache_load.wait()
    summed = jnp.zeros((PAIR, row_width), F32)
    pad = jnp.zeros((PAIR - RQ, BLK), F32)
    for r in range(RQ):
        own = jnp.where(request_sub == r, dropped, 0.0)
        both = jnp.concatenate([picks[r], own, pad], axis=0).astype(BF16)
        chosen = lax.dot_general(both, cache[r], contract, preferred_element_type=F32)
        summed = summed + chosen[KB:]
        chosen = chosen[:KB]
        kept[r] = chosen.astype(BF16)
        for i in range(LAT // LANES):
            piece = chosen[:, i * LANES : (i + 1) * LANES]
            blocks[r, i * KB : (i + 1) * KB, :] = piece.astype(BF16)
        rope = chosen[:, LAT:]
        rope = jnp.concatenate([rope[: KB // 2], rope[KB // 2 :]], axis=1)
        blocks[r, ROPE_AT:SUMM_AT, :] = rope.astype(BF16)
    mass_pair = jnp.concatenate([mass, jnp.ones_like(mass)], axis=0)
    summary = (summed / mass_pair).astype(BF16)
    summ[...] = summary
    summary_f = summary.astype(F32)[:RQ]
    summary_f = jnp.concatenate(
        [summary_f, jnp.zeros((RQ, 5 * LANES - row_width), F32)], axis=1
    )
    line = lax.broadcasted_iota(jnp.int32, (PAIR, LANES), 0)
    for r in range(RQ):
        lines = jnp.zeros((PAIR, LANES), F32)
        for i in range(5):
            piece = summary_f[r : r + 1, i * LANES : (i + 1) * LANES]
            lines = jnp.where(line == i, jnp.broadcast_to(piece, (PAIR, LANES)), lines)
        blocks[r, SUMM_AT:, :] = lines.astype(BF16)

    dest_load.wait()
    owners = [dest_ref[r, me] >> 2 for r in range(RQ)]

    def request_for(owner):
        chosen = jnp.int32(0)
        for r in range(RQ):
            chosen = jnp.where(owners[r] == owner, jnp.int32(r), chosen)
        return chosen

    block_recv[me] = blocks[request_for(me)]
    for k in range(1, seq_count):
        block_send[k - 1] = blocks[request_for(seq_peer(k))]

    def start_pack(k):
        return to_peer(
            block_send.at[k - 1],
            block_recv.at[me],
            r_send.at[k - 1],
            r_recv.at[k - 1],
            (seq_peer(k), my_mp),
        )

    far = seq_count // 2
    early = (far, 1, seq_count - 1)
    pack_copies = [start_pack(k) for k in early]

    absorb_load.wait()
    for copy in query_copies:
        copy.wait_recv()
    first_half = lax.broadcasted_iota(jnp.int32, (PAIR, NOPE), 0) < RQ
    for s in range(seq_count):
        part = query_recv[s]
        nope = part[:, :NOPE].astype(F32)
        split = jnp.concatenate(
            [jnp.where(first_half, nope, 0.0), jnp.where(first_half, 0.0, nope)], axis=1
        ).astype(BF16)
        weight = absorb_w[2 * s : 2 * s + 2].reshape(2 * NOPE, LAT)
        latent = jnp.dot(split, weight, preferred_element_type=F32).astype(BF16)
        query_flat[PAIR * s : PAIR * (s + 1), :LAT] = latent
        query_flat[PAIR * s : PAIR * (s + 1), LAT:] = part[:, NOPE:]

    rows = H * RQ
    score_scale = (NOPE + ROPE) ** (-0.5)
    flat = query_flat[...]
    kept_all = kept[...].reshape(RQ * KB, row_width)
    row_scores = lax.dot_general(flat, kept_all, contract, preferred_element_type=F32)
    summ_scores = lax.dot_general(flat, summ[...], contract, preferred_element_type=F32)
    row_request = lax.broadcasted_iota(jnp.int32, (rows, RQ * KB), 0) & (RQ - 1)
    col_request = lax.broadcasted_iota(jnp.int32, (rows, RQ * KB), 1) // KB
    row_scores = jnp.where(row_request == col_request, row_scores * score_scale, NEGATIVE)
    summ_request = lax.broadcasted_iota(jnp.int32, (rows, PAIR), 0) & (RQ - 1)
    summ_column = lax.broadcasted_iota(jnp.int32, (rows, PAIR), 1)
    summ_scores = summ_scores * score_scale + jnp.log(F32(BLK - KB))
    summ_scores = jnp.where(summ_request == summ_column, summ_scores, NEGATIVE)
    maxima = jnp.maximum(
        jnp.max(row_scores, axis=1, keepdims=True), jnp.max(summ_scores, axis=1, keepdims=True)
    )
    row_weights = jnp.exp(row_scores - maxima)
    summ_weights = jnp.exp(summ_scores - maxima)
    totals = jnp.sum(row_weights, axis=1, keepdims=True) + jnp.sum(
        summ_weights, axis=1, keepdims=True
    )
    weighted = jnp.dot(
        row_weights.astype(BF16), kept_all[:, :LAT], preferred_element_type=F32
    ) + jnp.dot(summ_weights.astype(BF16), summ[:, :LAT], preferred_element_type=F32)
    live_rows = lax.broadcasted_iota(jnp.int32, (rows, 128), 0) & (RQ - 1)
    level = jnp.broadcast_to(maxima + jnp.log(totals), (rows, 128))
    for r in range(RQ):
        level = jnp.where((live_rows == r) & (owners[r] < 0), NEGATIVE, level)
    high = level.astype(BF16).astype(F32)
    middle = (level - high).astype(BF16).astype(F32)
    low = level - high - middle
    lane = lax.broadcasted_iota(jnp.int32, (rows, 128), 1)
    terms = jnp.where(
        lane == 0, high, jnp.where(lane == 1, middle, jnp.where(lane == 2, low, 0.0))
    )
    part_send[:, :, :LAT] = (weighted / totals).astype(BF16).reshape(seq_count, PAIR, LAT)
    part_send[:, :, LAT:] = terms.astype(BF16).reshape(seq_count, PAIR, 128)
    part_copies = [
        to_peer(
            part_send.at[seq_peer(k)],
            part_recv.at[me],
            p_send.at[k - 1],
            p_recv.at[k - 1],
            (seq_peer(k), my_mp),
        )
        for k in range(1, seq_count)
    ]
    part_recv[me] = part_send[me]

    ranges_load.wait()
    ids_load.wait()
    total_rows = mp_count * RQ
    window_row = lax.broadcasted_iota(jnp.int32, (total_rows, 128), 0)
    window_low = jnp.zeros((total_rows, 128), jnp.int32)
    window_high = jnp.zeros((total_rows, 128), jnp.int32)
    for row in range(total_rows):
        tenant = ids_ref[row]
        window_low = jnp.where(window_row == row, ranges_ref[0, tenant], window_low)
        window_high = jnp.where(window_row == row, ranges_ref[1, tenant], window_high)
    vocab_start = (me * mp_count + my_mp) * vocab_width
    window_low = window_low - vocab_start
    window_high = window_high - vocab_start

    slot_source = [jnp.int32(0)] * slot_count
    for r in range(RQ):
        for b in range(block_count):
            offset = dest_ref[r, b] - me * slot_count
            for j in range(slot_count):
                slot_source[j] = jnp.where(offset == j, jnp.int32(b), slot_source[j])

    up_load.wait()
    for copy in part_copies:
        copy.wait_recv()
    levels = [
        jnp.sum(part_recv[s, :, LAT:].astype(F32), axis=1, keepdims=True)
        for s in range(seq_count)
    ]
    peak = functools.reduce(jnp.maximum, levels)
    factors = [jnp.exp(part_level - peak) for part_level in levels]
    merged_sum = functools.reduce(
        jnp.add, [factors[s] * part_recv[s, :, :LAT].astype(F32) for s in range(seq_count)]
    )
    attended = (merged_sum / functools.reduce(jnp.add, factors)).astype(BF16).astype(F32)
    first_wide = lax.broadcasted_iota(jnp.int32, (PAIR, LAT), 0) < RQ
    split = jnp.concatenate(
        [jnp.where(first_wide, attended, 0.0), jnp.where(first_wide, 0.0, attended)], axis=1
    ).astype(BF16)
    values = jnp.dot(split, up_w[...].reshape(2 * LAT, VH), preferred_element_type=F32)
    value_recv[me] = values.astype(BF16)
    value_copies = [
        to_peer(
            value_recv.at[me],
            value_recv.at[me],
            v_send.at[k - 1],
            v_recv.at[k - 1],
            (seq_peer(k), my_mp),
        )
        for k in range(1, seq_count)
    ]
    out_load.wait()
    for copy in value_copies:
        copy.wait_recv()
    all_values = jnp.concatenate(
        [unfold(value_recv[s]) for s in range(seq_count)], axis=1
    ).astype(BF16)
    col_width = out_w.shape[1]
    residual = hidden_ref[:, pl.ds(pl.multiple_of(me * col_width, 128), col_width)]
    hidden = residual.astype(F32) + jnp.dot(all_values, out_w[...], preferred_element_type=F32)
    hidden = hidden.astype(BF16)
    hidden_out[...] = hidden

    def store(i, src, dst):
        copy = pltpu.make_async_copy(src, dst, store_sem.at[i])
        copy.start()
        return copy

    stores = [store(0, hidden_out, hidden_out_hbm)]
    hidden_all[my_mp, me] = fold(hidden.astype(F32)).astype(BF16)

    hidden_copies = [
        to_peer(
            hidden_all.at[my_mp, me],
            hidden_all.at[my_mp, me],
            h_send.at[k - 1],
            h_recv.at[k - 1],
            (seq_peer(k), my_mp),
        )
        for k in range(1, seq_count)
    ]
    for copy in hidden_copies:
        copy.wait_recv()
    group_copies = [
        to_peer(
            hidden_all.at[my_mp],
            hidden_all.at[my_mp],
            g_send.at[k - 1],
            g_recv.at[k - 1],
            (me, mp_peer(k)),
        )
        for k in range(1, mp_count)
    ]
    own_rows = jnp.concatenate(
        [unfold(hidden_all[my_mp, s]) for s in range(seq_count)], axis=1
    )
    own_norm = jnp.sqrt(jnp.mean(own_rows * own_rows, axis=1, keepdims=True))
    norm_out[...] = as_row(own_norm)
    stores.append(store(1, norm_out, norm_hbm))
    gain_load.wait()
    gain = gain_ref[...].astype(F32).reshape(1, -1)
    for copy in group_copies:
        copy.wait_recv()
    pack_copies += [start_pack(k) for k in range(1, seq_count) if k not in early]
    normed = []
    for m in range(mp_count):
        group = jnp.concatenate([unfold(hidden_all[m, s]) for s in range(seq_count)], axis=1)
        mean_sq = jnp.mean(group * group, axis=1, keepdims=True)
        normed.append(group * lax.rsqrt(mean_sq + 1e-06) * gain)
    normed = jnp.concatenate(normed, axis=0).astype(BF16)

    head_load.wait()
    lane = lax.broadcasted_iota(jnp.int32, (total_rows, 128), 1)

    def head_step(n, best):
        start = pl.multiple_of(n * tile, 128)
        logits = jnp.dot(normed, head_w[:, pl.ds(start, tile)], preferred_element_type=F32)
        for i in range(tile // 128):
            column = lane + (start + i * 128)
            allowed = (column >= window_low) & (column < window_high)
            best = jnp.maximum(
                best, jnp.where(allowed, logits[:, i * 128 : (i + 1) * 128], NEGATIVE)
            )
        return best

    best = lax.fori_loop(
        0, vocab_width // tile, head_step, jnp.full((total_rows, 128), NEGATIVE, F32)
    )
    best = jnp.broadcast_to(jnp.max(best, axis=1, keepdims=True), (total_rows, 128))
    diagonal = window_row == lane
    here = me * mp_count + my_mp
    best_all[here] = jnp.sum(jnp.where(diagonal, best, 0.0), axis=0, keepdims=True)
    best_copies = [
        to_peer(
            best_all.at[here], best_all.at[here], b_send.at[k - 1], b_recv.at[k - 1], other(k)
        )
        for k in range(1, device_count)
    ]

    for copy in pack_copies:
        copy.wait_recv()
    lines = []
    for j in range(slot_count):
        source = slot_source[j]
        block = block_recv[source]
        for i in range(LAT // LANES):
            rows_out[j, :, i * LANES : (i + 1) * LANES] = block[i * KB : (i + 1) * KB]
        rope = block[ROPE_AT:SUMM_AT].astype(F32)
        rope = jnp.concatenate([rope[:, :ROPE], rope[:, ROPE:]], axis=0)
        rows_out[j, :, LAT:] = rope.astype(BF16)
        tail = block[SUMM_AT:].astype(F32)
        line = jnp.concatenate([tail[i : i + 1] for i in range(5)], axis=1)
        lines.append(line[:, :row_width])
    summary_out[...] = jnp.concatenate(lines, axis=0).astype(BF16)
    stores.append(store(2, rows_out, rows_hbm))
    stores.append(store(3, summary_out, summary_hbm))

    for copy in best_copies:
        copy.wait_recv()
    top = jnp.max(best_all[...], axis=0)
    own_top = top[:, :RQ]
    for m in range(1, mp_count):
        own_top = jnp.where(my_mp == m, top[:, m * RQ : (m + 1) * RQ], own_top)
    top_out[...] = own_top
    stores.append(store(4, top_out, top_hbm))
    for copy in (
        query_copies
        + pack_copies
        + part_copies
        + value_copies
        + hidden_copies
        + group_copies
        + best_copies
    ):
        copy.wait_send()
    for copy in stores:
        copy.wait()


def publish_kernel(*refs):
    results, places, staged = refs[:5], refs[5:10], refs[10:15]
    in_sem, out_sem = refs[15:]
    loads = [
        pltpu.make_async_copy(result, stage, in_sem.at[i])
        for i, (result, stage) in enumerate(zip(results, staged))
    ]
    stores = [
        pltpu.make_async_copy(stage, place, out_sem.at[i])
        for i, (stage, place) in enumerate(zip(staged, places))
    ]
    for copy in loads:
        copy.start()
    for load, store in zip(loads, stores):
        load.wait()
        store.start()
    for copy in stores:
        copy.wait()


def fused_body(
    hidden_in,
    query_weight,
    key_absorb,
    value_up,
    out_weight,
    latent_cache,
    cache_lengths,
    keep_lists,
    drop_weights,
    pack_dest,
    final_gain,
    head_weight,
    tenant_ranges,
    tenant_ids,
):
    seq_count = lax.axis_size("seq")
    mp_count = lax.axis_size("mp")
    row_width = LAT + ROPE
    slot_count = RQ // 2
    depth, vocab_width = head_weight.shape
    tile = next(t for t in (640, 512, 384, 256, 128) if vocab_width % t == 0)
    hbm = pl.BlockSpec(memory_space=pltpu.HBM)
    seq_sems = pltpu.SemaphoreType.DMA((seq_count - 1,))
    all_sems = pltpu.SemaphoreType.DMA((seq_count * mp_count - 1,))
    mp_sems = pltpu.SemaphoreType.DMA((mp_count - 1,))
    outs = pl.pallas_call(
        functools.partial(layer_kernel, seq_count, mp_count, vocab_width, tile),
        out_shape=(
            jax.ShapeDtypeStruct((slot_count, KB, row_width), BF16),
            jax.ShapeDtypeStruct((slot_count, row_width), BF16),
            jax.ShapeDtypeStruct((RQ, out_weight.shape[1]), BF16),
            jax.ShapeDtypeStruct((1, RQ), F32),
            jax.ShapeDtypeStruct((1, RQ), F32),
        ),
        in_specs=[hbm] * 13,
        out_specs=(hbm,) * 5,
        scratch_shapes=[
            pltpu.VMEM(hidden_in.shape, BF16),
            pltpu.VMEM(keep_lists.shape, jnp.int32),
            pltpu.VMEM(drop_weights.shape, jnp.int32),
            pltpu.VMEM(final_gain.shape, BF16),
            pltpu.SMEM(pack_dest.shape, jnp.int32),
            pltpu.SMEM((2, TENANTS), jnp.int32),
            pltpu.SMEM(tenant_ids.shape, jnp.int32),
            pltpu.VMEM((slot_count, KB, row_width), BF16),
            pltpu.VMEM((slot_count, row_width), BF16),
            pltpu.VMEM((RQ, out_weight.shape[1]), BF16),
            pltpu.VMEM((1, RQ), F32),
            pltpu.VMEM((1, RQ), F32),
            pltpu.VMEM(query_weight.shape, BF16),
            pltpu.VMEM(key_absorb.shape, BF16),
            pltpu.VMEM((2,) + value_up.shape[1:], BF16),
            pltpu.VMEM(out_weight.shape, BF16),
            pltpu.VMEM((RQ, row_width, BLK), BF16),
            pltpu.VMEM(head_weight.shape, BF16),
            pltpu.VMEM((seq_count, PAIR, NOPE + ROPE), BF16),
            pltpu.VMEM((H * RQ, row_width), BF16),
            pltpu.VMEM((RQ, KB, row_width), BF16),
            pltpu.VMEM((PAIR, row_width), BF16),
            pltpu.VMEM((RQ, MESSAGE, LANES), BF16),
            pltpu.VMEM((seq_count - 1, MESSAGE, LANES), BF16),
            pltpu.VMEM((seq_count, MESSAGE, LANES), BF16),
            pltpu.VMEM((seq_count, PAIR, LAT + 128), BF16),
            pltpu.VMEM((seq_count, PAIR, LAT + 128), BF16),
            pltpu.VMEM((seq_count, PAIR, VH), BF16),
            pltpu.VMEM((mp_count, seq_count, PAIR, out_weight.shape[1] // 2), BF16),
            pltpu.VMEM((seq_count * mp_count, 1, 128), F32),
            pltpu.SemaphoreType.DMA((13,)),
            pltpu.SemaphoreType.DMA((5,)),
        ]
        + [seq_sems] * 10
        + [mp_sems] * 2
        + [all_sems] * 2,
        compiler_params=pltpu.CompilerParams(
            collective_id=0, has_side_effects=True, vmem_limit_bytes=60 * 2**20
        ),
    )(
        hidden_in,
        keep_lists,
        drop_weights,
        final_gain,
        pack_dest,
        jnp.swapaxes(tenant_ranges, 0, 1),
        tenant_ids,
        query_weight,
        key_absorb,
        value_up,
        out_weight,
        jnp.swapaxes(latent_cache, 1, 2),
        head_weight,
    )
    outs = pl.pallas_call(
        publish_kernel,
        out_shape=tuple(jax.ShapeDtypeStruct(out.shape, out.dtype) for out in outs),
        in_specs=[hbm] * 5,
        out_specs=(hbm,) * 5,
        scratch_shapes=[pltpu.VMEM(out.shape, out.dtype) for out in outs]
        + [pltpu.SemaphoreType.DMA((5,))] * 2,
        compiler_params=pltpu.CompilerParams(vmem_limit_bytes=60 * 2**20),
    )(*outs)
    packed_rows, packed_summary, hidden_out, state_norm, top_logit = outs
    return (
        packed_rows,
        packed_summary,
        hidden_out,
        state_norm.reshape(RQ),
        top_logit.reshape(RQ),
    )


def solution(mesh):
    in_specs = (
        P("mp", None),
        P(None, "seq"),
        P(),
        P(),
        P(None, "seq"),
        P("mp", "seq", None),
        P("mp"),
        P("mp", "seq", None),
        P("mp", "seq"),
        P("mp", None),
        P(),
        P(None, ("seq", "mp")),
        P(),
        P(),
    )
    out_specs = (
        P(("seq", "mp"), None, None),
        P(("seq", "mp"), None),
        P("mp", "seq"),
        P("mp"),
        P("mp"),
    )
    seq_count = mesh.shape["seq"]
    fused = seq_count * 2 == H
    return jax.shard_map(fused_body if fused else body, mesh=mesh, in_specs=in_specs, out_specs=out_specs, check_vma=False)
```
